256 devices in a mesh: dp: 8 (over y, x_hi), seq: 32 (over x_lo, z, core).
Axes of the slice: x: 4 (x_hi: 2, x_lo: 2; x = x_hi * 2 + x_lo), y: 4, z: 8, core: 2. Of those that a mesh axis runs over, the one named last changes fastest.
Arguments:
- tiles: bfloat16 [8, 16384, 768], P('dp', 'seq'), may hold values from -6 to 6
- cotangent: bfloat16 [8, 16384, 768], P('dp', 'seq'), may hold values from -192 to 192
- gain: bfloat16 [768], replicated, may hold values from 0.5 to 1.5
- query_matrix: bfloat16 [768, 768], replicated, may hold values from -0.21875 to 0.21875
- key_matrix: bfloat16 [768, 768], replicated, may hold values from -0.21875 to 0.21875
- value_matrix: bfloat16 [768, 768], replicated, may hold values from -0.21875 to 0.21875
- w_out: bfloat16 [768, 768], replicated, may hold values from -0.21875 to 0.21875
- query_down_factor: bfloat16 [768, 8], replicated, may hold values from -0.21875 to 0.21875
- query_up_factor: bfloat16 [8, 768], replicated, may hold values from -1.1953125 to 1.1953125
- value_down_factor: bfloat16 [768, 8], replicated, may hold values from -0.21875 to 0.21875
- value_up_factor: bfloat16 [8, 768], replicated, may hold values from -1.1953125 to 1.1953125
- valid_count: int32 [8], P('dp'), may hold values from 8192 to 16384, as said below
Outputs:
- incoming_derivative: bfloat16 [8, 16384, 768], P('dp', 'seq')
- adapter_grads: float32 [4, 8, 768], replicated
The draws below stay inside these ranges and needn't reach their ends.
Inputs may be any that keep to these rules, and one draw needn't show every extreme that they name: `valid_count`: each slide has at least half of its tiles valid, and in every draw some slide is entirely valid.
All inputs are finite; a program needn't handle non-finite values.
Results may differ from the reference program's by a relative error of at most 0.02.
Values may be sent and summed in bfloat16 or wider, within the bound.
A program may use at most 128 MiB of HBM per device.

```python
import math
import jax
import jax.numpy as jnp
from jax import lax

D = 768
HEAD_COUNT = 16
HEAD_WIDTH = 48
R = 8
DEVICE_TILES = 512
FINE_SEGMENT0 = 512
MIDDLE_DILATION = 4
COARSE_DILATION = 32
PATCHES_PER_WSI = 16384
SPECIMEN_IMAGES = 8
N_SEQ = 32


def draw_valid_count(key, part):
    key = jax.random.fold_in(key, 7)
    first, second = jax.random.split(key)
    short = jax.random.randint(first, (SPECIMEN_IMAGES,), 0, PATCHES_PER_WSI // 2 + 1)
    full = jax.random.randint(second, (), 0, SPECIMEN_IMAGES)
    return jnp.where(jnp.arange(SPECIMEN_IMAGES) == full, PATCHES_PER_WSI, PATCHES_PER_WSI - short).astype(jnp.int32)


def steps_of(own_key, extent, shards, smallest, high):
    def one(axis_at, shards_of):
        draws = jax.random.uniform(jax.random.fold_in(jax.random.fold_in(own_key, 6), axis_at), (shards_of,), jnp.float32, smallest / len(shards), high / len(shards))
        return jnp.repeat(jnp.exp(draws), extent[axis_at] // shards_of).reshape((-1,) + (1,) * (len(extent) - axis_at - 1))

    level = one(*shards[0])
    for cut in shards[1:]:
        level = level * one(*cut)
    return level


def scatter_about(key, extent, deviation, most, cuts=(), kind=jnp.bfloat16):
    values = jax.random.normal(key, extent, jnp.float32) * deviation
    if len(cuts) > 0:
        values = steps_of(key, extent, cuts, -0.22, 0.18) * values
    return jnp.clip(values, min=-most, max=most).astype(kind)


def setup_inputs(seed: int = 0) -> dict:
    keys = jax.random.split(jax.random.key(seed), 13)
    tiles = scatter_about(keys[0], (SPECIMEN_IMAGES, PATCHES_PER_WSI, D), 1.0, 6.0, ((0, 8), (1, 32)))
    cotangent = scatter_about(keys[1], (SPECIMEN_IMAGES, PATCHES_PER_WSI, D), 32.0, 192.0, ((0, 8), (1, 32)))
    gain = jnp.clip(1.0 + 0.1 * jax.random.normal(keys[2], (D,), jnp.float32), 0.5, 1.5).astype(jnp.bfloat16)
    query_matrix = scatter_about(keys[3], (D, D), D ** -0.5, 0.21875)
    key_matrix = scatter_about(keys[4], (D, D), D ** -0.5, 0.21875)
    value_matrix = scatter_about(keys[5], (D, D), D ** -0.5, 0.21875)
    w_out = scatter_about(keys[6], (D, D), D ** -0.5, 0.21875)
    query_down_factor = scatter_about(keys[7], (D, R), D ** -0.5, 0.21875)
    query_up_factor = scatter_about(keys[8], (R, D), 0.2, 1.1953125)
    value_down_factor = scatter_about(keys[9], (D, R), D ** -0.5, 0.21875)
    value_up_factor = scatter_about(keys[10], (R, D), 0.2, 1.1953125)
    valid_count = draw_valid_count(jax.random.fold_in(keys[12], 71), 0)
    return {"tiles": tiles, "cotangent": cotangent, "gain": gain, "query_matrix": query_matrix, "key_matrix": key_matrix, "value_matrix": value_matrix, "w_out": w_out, "query_down_factor": query_down_factor, "query_up_factor": query_up_factor, "value_down_factor": value_down_factor, "value_up_factor": value_up_factor, "valid_count": valid_count}


adapter_scale = 2.0
eps = 1e-05

def layer_normalize(tiles):
    payload_vectors = tiles.astype(jnp.float32)
    center = payload_vectors - lax.optimization_barrier(jnp.mean(payload_vectors, -1, keepdims=True))
    inverse_deviation = lax.rsqrt(lax.optimization_barrier(jnp.mean(center * center, -1, keepdims=True)) + eps)
    return (center * inverse_deviation, inverse_deviation)

def allowed_keys(query_pos, key_pos, valid):
    return (key_pos[..., None, :] < valid) | (key_pos[..., None, :] == query_pos[..., :, None])

def exponentials(probe_embeddings, address_embeddings, allowed):
    softmax_sharpness = 1.0 / math.sqrt(probe_embeddings.shape[-1])
    similarity_grid = jnp.einsum('qir,bir->iqb', probe_embeddings.astype(jnp.float32), address_embeddings.astype(jnp.float32)) * softmax_sharpness
    return jnp.where(allowed[None, :, :], jnp.exp(similarity_grid), 0.0)

def weights_of(expo, total_sum):
    return (expo / total_sum[:, :, None]).astype(jnp.bfloat16)

def value_mixing(probabilities, payload_vectors):
    return jnp.einsum('ist,tie->sie', probabilities.astype(jnp.float32), payload_vectors.astype(jnp.float32))

def score_grads(expo, total_sum, row_delta, result_cotangent, payload_vectors):
    weighting_cotangent = jnp.einsum('qir,bir->iqb', result_cotangent.astype(jnp.float32), payload_vectors.astype(jnp.float32))
    return (expo / total_sum[:, :, None] * (weighting_cotangent - row_delta[:, :, None])).astype(jnp.bfloat16)

def query_gradients(derivative_sequence, address_embeddings):
    softmax_sharpness = 1.0 / math.sqrt(address_embeddings.shape[-1])
    return jnp.einsum('ist,tie->sie', derivative_sequence.astype(jnp.float32), address_embeddings.astype(jnp.float32)) * softmax_sharpness

def key_grads(derivative_sequence, probe_embeddings):
    softmax_sharpness = 1.0 / math.sqrt(probe_embeddings.shape[-1])
    return jnp.einsum('oig,ioe->goe', derivative_sequence.astype(jnp.float32), probe_embeddings.astype(jnp.float32)) * softmax_sharpness

def value_grads(probabilities, result_cotangent):
    return jnp.einsum('oig,ioe->goe', probabilities.astype(jnp.float32), result_cotangent.astype(jnp.float32))

def slide_backward(tiles, cotangent, valid, gain, query_matrix, key_matrix, value_matrix, w_out, query_down_factor, query_up_factor, value_down_factor, value_up_factor):
    highest_precision = lax.Precision.HIGHEST
    centered_input, inverse_deviation = layer_normalize(tiles)
    normed_input = (centered_input * gain.astype(jnp.float32)).astype(jnp.bfloat16)
    query_lift = jnp.dot(normed_input, query_down_factor, preferred_element_type=jnp.float32)
    value_lift = jnp.dot(normed_input, value_down_factor, preferred_element_type=jnp.float32)
    probe_embeddings = (jnp.dot(normed_input, query_matrix, preferred_element_type=jnp.float32) + adapter_scale * jnp.dot(query_lift, query_up_factor.astype(jnp.float32), precision=highest_precision)).astype(jnp.bfloat16).reshape(PATCHES_PER_WSI, HEAD_COUNT, HEAD_WIDTH)
    address_embeddings = jnp.dot(normed_input, key_matrix, preferred_element_type=jnp.float32).astype(jnp.bfloat16).reshape(PATCHES_PER_WSI, HEAD_COUNT, HEAD_WIDTH)
    payload_vectors = (jnp.dot(normed_input, value_matrix, preferred_element_type=jnp.float32) + adapter_scale * jnp.dot(value_lift, value_up_factor.astype(jnp.float32), precision=highest_precision)).astype(jnp.bfloat16).reshape(PATCHES_PER_WSI, HEAD_COUNT, HEAD_WIDTH)
    attention_gradient = jnp.dot(cotangent, w_out.T, preferred_element_type=jnp.float32).astype(jnp.bfloat16).reshape(PATCHES_PER_WSI, HEAD_COUNT, HEAD_WIDTH)
    token_positions = jnp.arange(PATCHES_PER_WSI, dtype=jnp.int32)
    group_count = (token_positions.reshape(PATCHES_PER_WSI // FINE_SEGMENT0, FINE_SEGMENT0), token_positions[::MIDDLE_DILATION].reshape(N_SEQ // 2, 2 * DEVICE_TILES // MIDDLE_DILATION), token_positions[::COARSE_DILATION].reshape(1, PATCHES_PER_WSI // COARSE_DILATION))
    total_sum = jnp.zeros((PATCHES_PER_WSI, HEAD_COUNT), jnp.float32)
    for group in group_count:

        def sums(member):
            expo = exponentials(probe_embeddings[member], address_embeddings[member], allowed_keys(member, member, valid))
            return lax.optimization_barrier(jnp.sum(expo, -1)).T
        total_sum = total_sum.at[group.reshape(-1)].add(lax.map(sums, group).reshape(-1, HEAD_COUNT))
    mixed_output = jnp.zeros((PATCHES_PER_WSI, HEAD_COUNT, HEAD_WIDTH), jnp.float32)
    for group in group_count:

        def mix(member):
            expo = exponentials(probe_embeddings[member], address_embeddings[member], allowed_keys(member, member, valid))
            return value_mixing(weights_of(expo, total_sum[member].T), payload_vectors[member])
        mixed_output = mixed_output.at[group.reshape(-1)].add(lax.map(mix, group).reshape(-1, HEAD_COUNT, HEAD_WIDTH))
    attended = mixed_output.astype(jnp.bfloat16)
    row_delta = lax.optimization_barrier(jnp.sum(attention_gradient.astype(jnp.float32) * attended.astype(jnp.float32), -1))
    query_gradient = jnp.zeros((PATCHES_PER_WSI, HEAD_COUNT, HEAD_WIDTH), jnp.float32)
    key_gradient = jnp.zeros((PATCHES_PER_WSI, HEAD_COUNT, HEAD_WIDTH), jnp.float32)
    value_gradient = jnp.zeros((PATCHES_PER_WSI, HEAD_COUNT, HEAD_WIDTH), jnp.float32)
    for group in group_count:

        def back(member):
            expo = exponentials(probe_embeddings[member], address_embeddings[member], allowed_keys(member, member, valid))
            row_total = total_sum[member].T
            probabilities = weights_of(expo, row_total)
            derivative_sequence = score_grads(expo, row_total, row_delta[member].T, attention_gradient[member], payload_vectors[member])
            return (query_gradients(derivative_sequence, address_embeddings[member]), key_grads(derivative_sequence, probe_embeddings[member]), value_grads(probabilities, attention_gradient[member]))
        part_q, part_k, part_v = lax.map(back, group)
        flat = group.reshape(-1)
        query_gradient = query_gradient.at[flat].add(part_q.reshape(-1, HEAD_COUNT, HEAD_WIDTH))
        key_gradient = key_gradient.at[flat].add(part_k.reshape(-1, HEAD_COUNT, HEAD_WIDTH))
        value_gradient = value_gradient.at[flat].add(part_v.reshape(-1, HEAD_COUNT, HEAD_WIDTH))
    rounded_queries = query_gradient.astype(jnp.bfloat16).reshape(PATCHES_PER_WSI, D)
    rounded_keys = key_gradient.astype(jnp.bfloat16).reshape(PATCHES_PER_WSI, D)
    rounded_values = value_gradient.astype(jnp.bfloat16).reshape(PATCHES_PER_WSI, D)
    query_return = jnp.dot(rounded_queries, query_up_factor.T, preferred_element_type=jnp.float32)
    value_return = jnp.dot(rounded_values, value_up_factor.T, preferred_element_type=jnp.float32)
    normed_gradient = jnp.dot(rounded_queries, query_matrix.T, preferred_element_type=jnp.float32) + jnp.dot(rounded_keys, key_matrix.T, preferred_element_type=jnp.float32) + jnp.dot(rounded_values, value_matrix.T, preferred_element_type=jnp.float32) + adapter_scale * jnp.dot(query_return, query_down_factor.astype(jnp.float32).T, precision=highest_precision) + adapter_scale * jnp.dot(value_return, value_down_factor.astype(jnp.float32).T, precision=highest_precision)
    scaled_scores = normed_gradient * gain.astype(jnp.float32)
    incoming_derivative = inverse_deviation * (scaled_scores - lax.optimization_barrier(jnp.mean(scaled_scores, -1, keepdims=True)) - centered_input * lax.optimization_barrier(jnp.mean(scaled_scores * centered_input, -1, keepdims=True)))
    normed_widened = normed_input.astype(jnp.float32)
    low_rank_couplets = jnp.stack([adapter_scale * jnp.dot(query_return.T, normed_widened, precision=highest_precision), adapter_scale * jnp.dot(query_lift.T, rounded_queries.astype(jnp.float32), precision=highest_precision), adapter_scale * jnp.dot(value_return.T, normed_widened, precision=highest_precision), adapter_scale * jnp.dot(value_lift.T, rounded_values.astype(jnp.float32), precision=highest_precision)])
    return (incoming_derivative.astype(jnp.bfloat16), low_rank_couplets)

def reference(tiles, cotangent, gain, query_matrix, key_matrix, value_matrix, w_out, query_down_factor, query_up_factor, value_down_factor, value_up_factor, valid_count):

    def one_slide(item):
        slide_tiles, slide_cot, valid = item
        return slide_backward(slide_tiles, slide_cot, valid, gain, query_matrix, key_matrix, value_matrix, w_out, query_down_factor, query_up_factor, value_down_factor, value_up_factor)
    incoming_derivative, low_rank_couplets = lax.map(one_slide, (tiles, cotangent, valid_count))
    softmax_sharpness = 1.0 / math.sqrt(SPECIMEN_IMAGES * PATCHES_PER_WSI)
    return (incoming_derivative, lax.optimization_barrier(jnp.sum(low_rank_couplets, 0)) * softmax_sharpness)
```

```python
import math

import jax
import jax.numpy as jnp
from jax import lax
from jax.experimental import pallas as pl
from jax.experimental.pallas import tpu as pltpu
from jax.sharding import PartitionSpec as P

T = 512
D = 768
H = 16
W = 48
R = 8
PAIR = 128
FAR = 16
SEQ = 32
DP = 8
CHIPS = 16
GROUPS = 2
SLICES = 12
PER = 8
EPS = 1e-5
LOG2E = math.log2(math.e)
SHARP = 1.0 / math.sqrt(W)
LN2 = math.log(2.0)
MESH = pl.DeviceIdType.MESH
f32 = jnp.float32
bf16 = jnp.bfloat16
VMEM_LIMIT = 56 * 1024 * 1024


def iota(shape, axis):
    return lax.broadcasted_iota(jnp.int32, shape, axis)


def dot(a, b):
    return jnp.dot(a, b, preferred_element_type=f32)


def dot_nt(a, b):
    return lax.dot_general(a, b, (((1,), (1,)), ((), ())), preferred_element_type=f32)


def place_of(row):
    return (row % 16) * 32 + ((row // 16) % 8) * 4 + row // 128


def order_matrix():
    return jnp.where(place_of(iota((T, T), 0)) == iota((T, T), 1), 1.0, 0.0).astype(bf16)


def halves(value):
    upper = value.astype(bf16)
    lower = (value - upper.astype(f32)).astype(bf16)
    return upper, lower


def normalize(x):
    center = x - jnp.mean(x, -1, keepdims=True)
    inverse = lax.rsqrt(jnp.mean(center * center, -1, keepdims=True) + EPS)
    return center * inverse, inverse


def window(hh):
    low = W * hh
    first = low // 128
    last = (low + W - 1) // 128
    return first * 128, (last - first + 1) * 128, low - first * 128


def lane_mask(width, off):
    lane = iota((1, width), 1)
    return jnp.where((lane >= off) & (lane < off + W), 1.0, 0.0).astype(bf16)


def pad_rows(block, off, width):
    parts = []
    if off:
        parts.append(jnp.zeros((off, block.shape[1]), block.dtype))
    parts.append(block)
    rest = width - off - block.shape[0]
    if rest:
        parts.append(jnp.zeros((rest, block.shape[1]), block.dtype))
    return jnp.concatenate(parts, 0)


def down_rows(qd_ref, vd_ref):
    return jnp.concatenate(
        [qd_ref[...].astype(f32), vd_ref[...].astype(f32), jnp.zeros((112, D), f32)], 0
    ).astype(bf16)


def up_padded(u_ref, at):
    return pad_rows(u_ref[...].astype(f32), at, 128).astype(bf16)


def layer_kernel(
    valid_ref, tiles_ref, cot_ref, gain_ref, wq_ref, wk_ref, wv_ref, wo_ref,
    qd_ref, qu_ref, vd_ref, vu_ref,
    out_ref, merged_ref,
    xhat_s, scale_s, normed_s, lift_s, q_ref, k_ref, v_ref, qt_ref, kt_ref, vt_ref, dat_ref,
    skv_ref, sqd_ref,
    e0, e1, mask0, mask1, tot, mix, dlt, dapt, dap, dqt, dq1t, dk, dv,
    k1, v1, k1t, v1t, dk1, dv1, gsend, gback,
    kv, qda, fe, send2, recv2, send3, recv3, skvg, sdq, rkvg, rdq,
    part, one, total, two, done,
    s_kv, r_kv, s_qd, r_qd, s_pair, r_pair, s_2, r_2, s_3, r_3, s_4, r_4, s_5, r_5, s_g, r_g,
    s_6, r_6, s_7, r_7, s_8, r_8,
):
    dp = lax.axis_index("dp")
    me = lax.axis_index("seq")
    chip = me // 2
    core = me % 2
    mate = chip * 2 + (1 - core)
    mine = me % 16
    half = me // 16
    plane = dp * 2 + half
    valid = valid_ref[0]

    def near_peer(j):
        return {"seq": half * 16 + (mine + j) % 16}

    def across_peer(j):
        other = (plane + j) % 16
        return {"dp": other // 2, "seq": (other % 2) * 16 + mine}

    barrier = pltpu.get_barrier_semaphore()

    def greet(j, carry):
        pl.semaphore_signal(
            barrier, inc=1, device_id={"seq": (me + j) % SEQ}, device_id_type=MESH
        )
        return carry

    def greet_across(j, carry):
        pl.semaphore_signal(barrier, inc=1, device_id=across_peer(j), device_id_type=MESH)
        return carry

    lax.fori_loop(1, SEQ, greet, 0)
    lax.fori_loop(1, 16, greet_across, 0)

    def remote_to(src, dst, send, recv, peer):
        return pltpu.make_async_remote_copy(
            src_ref=src, dst_ref=dst, send_sem=send, recv_sem=recv,
            device_id=peer, device_id_type=MESH,
        )

    def remote(src, dst, send, recv, peer):
        return remote_to(src, dst, send, recv, {"seq": peer})

    def drain(ref, sem):
        pltpu.make_async_copy(ref, ref, sem).wait()

    order = order_matrix()
    x = dot(order, tiles_ref[0])
    cot = dot(order, cot_ref[0]).astype(bf16)
    xhat, inverse_dev = normalize(x)
    xhat_s[...] = xhat
    scale_s[...] = jnp.broadcast_to(inverse_dev, (T, 128))
    normed = (xhat * gain_ref[...].astype(f32)).astype(bf16)
    normed_s[...] = normed
    down = down_rows(qd_ref, vd_ref)
    uq = up_padded(qu_ref, 0)
    uv = up_padded(vu_ref, R)
    lift = dot_nt(normed, down)
    both = jnp.concatenate(halves(lift), 1)
    lift_s[...] = lift.T[: 2 * R]
    q = dot(normed, wq_ref[...]) + 2.0 * dot(both, jnp.concatenate([uq, uq], 0))
    q = (q * (SHARP * LOG2E)).astype(bf16)
    q_ref[...] = q
    qt_ref[...] = q.T
    k = dot(normed, wk_ref[...]).astype(bf16)
    k_ref[...] = k
    kt_ref[...] = k.T
    v = (dot(normed, wv_ref[...]) + 2.0 * dot(both, jnp.concatenate([uv, uv], 0))).astype(bf16)
    v_ref[...] = v
    vt_ref[...] = v.T
    da = dot_nt(cot, wo_ref[...]).astype(bf16)
    dat_ref[...] = da.T
    gap = jnp.zeros((FAR, 64 - W), f32)
    qf, kf, vf, df = (rows[:FAR].astype(f32) for rows in (q, k, v, da))
    for h in range(H):
        cut = slice(W * h, W * h + W)
        skv_ref[h] = jnp.concatenate([kf[:, cut], gap, vf[:, cut], gap], 1).astype(bf16)
        sqd_ref[h] = jnp.concatenate([qf[:, cut], gap, df[:, cut], gap], 1).astype(bf16)

    pl.semaphore_wait(barrier, SEQ - 1 + 15)

    mine_rows = pl.ds(pl.multiple_of(core * 256 + chip * FAR, FAR), FAR)

    def slot(c):
        return pl.ds(pl.multiple_of(c * FAR, FAR), FAR)

    def send_same(j, carry):
        there = (chip + j) % CHIPS
        remote(skv_ref.at[there], kv.at[mine_rows], s_kv, r_kv, there * 2 + core).start()
        remote(sqd_ref.at[there], qda.at[slot(chip)], s_qd, r_qd, there * 2 + core).start()
        return carry

    def send_other(j, carry):
        there = (chip + j) % CHIPS
        remote(skv_ref.at[there], kv.at[mine_rows], s_kv, r_kv, there * 2 + (1 - core)).start()
        return carry

    lax.fori_loop(1, CHIPS, send_same, 0)
    lax.fori_loop(0, CHIPS, send_other, 0)
    pltpu.make_async_copy(skv_ref.at[chip], kv.at[mine_rows], r_kv).start()
    pltpu.make_async_copy(sqd_ref.at[chip], qda.at[slot(chip)], r_qd).start()

    near = pl.ds(0, PAIR)
    away = pl.ds(PAIR, PAIR)
    pair_copies = [
        remote(k_ref.at[near], k1.at[away], s_pair.at[0], r_pair.at[0], mate),
        remote(v_ref.at[near], v1.at[away], s_pair.at[1], r_pair.at[1], mate),
        remote(kt_ref.at[:, near], k1t.at[:, away], s_pair.at[2], r_pair.at[2], mate),
        remote(vt_ref.at[:, near], v1t.at[:, away], s_pair.at[3], r_pair.at[3], mate),
    ]
    for copy in pair_copies:
        copy.start()
    k1[near] = k_ref[near]
    v1[near] = v_ref[near]
    k1t[:, near] = kt_ref[:, near]
    v1t[:, near] = vt_ref[:, near]

    row = iota((T, T), 0)
    col = iota((T, T), 1)
    open0 = (me * T + place_of(row) < valid) | (row == col)
    mask0[...] = jnp.where(open0, jnp.inf, 0.0).astype(bf16)
    mask1[near] = mask0[near, near]
    row = iota((PAIR, PAIR), 0)
    mask1[away] = jnp.where(mate * T + place_of(row) < valid, jnp.inf, 0.0).astype(bf16)
    dk[...] = jnp.zeros_like(dk)
    dv[...] = jnp.zeros_like(dv)
    dk1[...] = jnp.zeros_like(dk1)
    dv1[...] = jnp.zeros_like(dv1)

    def place(g, hh):
        base, width, off = window(hh)
        lanes = pl.ds(pl.multiple_of(g * 384 + base, 128), width)
        rows = pl.ds(pl.multiple_of(g * 384 + W * hh, 16), W)
        return lanes, rows, width, off

    def forward(g, store, mask, keys, values_t, asks_t, out):
        totals = []
        for hh in range(PER):
            lanes, rows, width, off = place(g, hh)
            ask = pad_rows(asks_t(rows), off, width)
            expo = jnp.exp2(dot(keys(lanes), ask)).astype(bf16)
            expo = jnp.minimum(expo, mask[...])
            store[g * PER + hh] = expo
            value = values_t(rows)
            ones = jnp.ones((16, value.shape[1]), bf16)
            mixed = dot(jnp.concatenate([value, ones], 0), expo)
            totals.append(mixed[W : W + 1])
            out(rows, mixed[:W])
        return jnp.concatenate(totals, 0)

    def eight(g):
        return pl.ds(pl.multiple_of(g * PER, PER), PER)

    def forward0(g, carry):
        def put(rows, value):
            mix[rows, :] = value

        tot[eight(g), :] = forward(
            g, e0, mask0, lambda l: k_ref[:, l], lambda r: vt_ref[r, :], lambda r: qt_ref[r, :], put
        )
        return carry

    def forward1(g, carry):
        def put(rows, value):
            mix[rows, near] += value

        tot[eight(g), near] += forward(
            g, e1, mask1, lambda l: k1[:, l], lambda r: v1t[r, :], lambda r: qt_ref[r, near], put
        )
        return carry

    lax.fori_loop(0, 1, forward0, 0)

    drain(kv, r_kv)
    drain(qda, r_qd)
    lane = iota((1, 128), 1)
    low = jnp.where(lane < 64, 1.0, 0.0).astype(bf16)
    high = jnp.where(lane >= 64, 1.0, 0.0).astype(bf16)
    i2 = iota((256, T), 0)
    j2 = iota((256, T), 1)
    j2_pos = ((j2 % 256) // FAR * 2 + j2 // 256) * T + (j2 % FAR) * 32
    open2 = (j2_pos < valid) | (j2 == core * 256 + i2)
    far_expo = jnp.exp2(dot_nt(qda[...], kv[...] * low))
    far_expo = jnp.where(open2, far_expo, 0.0).astype(bf16)
    fe[...] = far_expo
    first_lane = jnp.where(lane == 0, 1.0, 0.0).astype(bf16)
    far_mixed = dot(far_expo, kv[...] * high + first_lane)
    far_r = jnp.sum(
        jnp.where(lane >= 64, qda[...].astype(f32) * far_mixed, 0.0), 1, keepdims=True
    )
    far_t = far_mixed[:, 0:1]
    send2[...] = jnp.where(lane == chip, far_t, 0.0) + jnp.where(lane == 64 + chip, far_r, 0.0)

    def send_totals(j, carry):
        there = (chip + j) % CHIPS
        remote(send2.at[slot(there)], recv2.at[slot(chip)], s_2, r_2, there * 2 + core).start()
        return carry

    lax.fori_loop(1, CHIPS, send_totals, 0)
    pltpu.make_async_copy(send2.at[slot(chip)], recv2.at[slot(chip)], r_2).start()

    lax.fori_loop(1, 2, forward0, 0)
    for copy in pair_copies:
        copy.wait()
    lax.fori_loop(0, GROUPS, forward1, 0)

    drain(recv2, r_2)
    gathered = recv2[pl.ds(0, FAR)]
    for c in range(1, CHIPS):
        gathered = gathered + recv2[pl.ds(c * FAR, FAR)]
    turned = jnp.concatenate([gathered, jnp.zeros((PAIR - FAR, 128), f32)], 0).T
    tot[:, near] += turned[:H]
    inverse = 1.0 / tot[...]
    tot[...] = inverse
    far_sums = jnp.concatenate([turned[64 : 64 + H], jnp.zeros((H, T - PAIR), f32)], 1)
    dlt[...] = far_sums * inverse * inverse
    for h in range(H):
        rows = pl.ds(W * h, W)
        this = tot[h : h + 1, :]
        scaled = (dat_ref[rows, :].astype(f32) * this).astype(bf16)
        dapt[rows, :] = scaled
        own = jnp.sum(scaled.astype(f32) * mix[rows, :], 0, keepdims=True)
        dlt[h : h + 1, :] += own * this
    filler = jnp.zeros((64 - H, 128), f32)
    send3[...] = jnp.concatenate([tot[:, near], filler, dlt[:, near], filler], 0).T[:FAR]

    def send_scales(j, carry):
        there = (chip + j) % CHIPS
        remote(send3, recv3.at[slot(chip)], s_3, r_3, there * 2 + core).start()
        return carry

    lax.fori_loop(1, CHIPS, send_scales, 0)
    pltpu.make_async_copy(send3, recv3.at[slot(chip)], r_3).start()
    dap[...] = dapt[...].T

    def backward(g, store, values, keys_t, grads, grads_t, deltas, out_q, out_v):
        for hh in range(PER):
            lanes, rows, width, off = place(g, hh)
            expo = store[g * PER + hh]
            dprob = dot(values(lanes), pad_rows(grads_t(rows), off, width))
            dscore = expo * (dprob - deltas(hh)).astype(bf16)
            store[g * PER + hh] = dscore
            out_q[rows, :] = dot(keys_t(rows), dscore)
            out_v[:, lanes] += dot(expo, grads(lanes) * lane_mask(width, off))

    def key_side(g, store, asks, out_k):
        for hh in range(PER):
            lanes, rows, width, off = place(g, hh)
            out_k[:, lanes] += dot(store[g * PER + hh], asks(lanes) * lane_mask(width, off))

    def backward0(g, carry):
        deltas = dlt[eight(g), :]
        backward(
            g, e0, lambda l: v_ref[:, l], lambda r: kt_ref[r, :], lambda l: dap[:, l],
            lambda r: dapt[r, :], lambda hh: deltas[hh : hh + 1], dqt, dv,
        )
        return carry

    def backward1(g, carry):
        deltas = dlt[eight(g), near]
        backward(
            g, e1, lambda l: v1[:, l], lambda r: k1t[r, :], lambda l: dap[near, l],
            lambda r: dapt[r, near], lambda hh: deltas[hh : hh + 1], dq1t, dv1,
        )
        key_side(g, e1, lambda l: q_ref[near, l], dk1)
        return carry

    def keys0(g, carry):
        key_side(g, e0, lambda l: q_ref[:, l], dk)
        return carry

    lax.fori_loop(0, GROUPS, backward1, 0)
    gsend[0] = dk1[away].astype(bf16)
    gsend[1] = dv1[away].astype(bf16)
    grad_copy = remote(gsend, gback, s_g, r_g, mate)
    grad_copy.start()
    lax.fori_loop(0, 1, backward0, 0)

    drain(recv3, r_3)
    scales = recv3[...]
    far_inv = jnp.sum(jnp.where(lane == chip, scales, 0.0), 1, keepdims=True)
    far_del = jnp.sum(jnp.where(lane == 64 + chip, scales, 0.0), 1, keepdims=True)
    far_grads = jnp.where(lane >= 64, qda[...].astype(f32) * far_inv, 0.0).astype(bf16)
    far_back = fe[...].astype(f32)
    far_ds = far_back * (dot_nt(far_grads, kv[...] * high) - far_del)
    sdq[...] = dot(far_ds.astype(bf16), kv[...] * low).astype(bf16)
    skvg[...] = (
        dot(far_ds.T.astype(bf16), qda[...] * low) + dot(far_back.T.astype(bf16), far_grads)
    ).astype(bf16)

    def return_same(j, carry):
        there = (chip + j) % CHIPS
        block = pl.ds(pl.multiple_of(core * 256 + there * FAR, FAR), FAR)
        remote(skvg.at[block], rkvg.at[mine_rows], s_4, r_4, there * 2 + core).start()
        remote(sdq.at[slot(there)], rdq.at[slot(chip)], s_5, r_5, there * 2 + core).start()
        return carry

    def return_other(j, carry):
        there = (chip + j) % CHIPS
        block = pl.ds(pl.multiple_of((1 - core) * 256 + there * FAR, FAR), FAR)
        remote(skvg.at[block], rkvg.at[mine_rows], s_4, r_4, there * 2 + (1 - core)).start()
        return carry

    lax.fori_loop(1, CHIPS, return_same, 0)
    lax.fori_loop(0, CHIPS, return_other, 0)
    pltpu.make_async_copy(skvg.at[mine_rows], rkvg.at[mine_rows], r_4).start()
    pltpu.make_async_copy(sdq.at[slot(chip)], rdq.at[slot(chip)], r_5).start()

    lax.fori_loop(1, 2, backward0, 0)

    grad_copy.wait()
    drain(rkvg, r_4)
    drain(rdq, r_5)
    keys_back, values_back, asks_back = [], [], []
    for h in range(H):
        here = rkvg[pl.ds(h * FAR, FAR)].astype(f32) + rkvg[pl.ds(256 + h * FAR, FAR)].astype(f32)
        keys_back.append(here[:, :W])
        values_back.append(here[:, 64 : 64 + W])
        asks_back.append(rdq[pl.ds(h * FAR, FAR)].astype(f32)[:, :W])
    few = pl.ds(0, FAR)
    dv[near] += dv1[near] + gback[1].astype(f32)
    dv[few] += jnp.concatenate(values_back, 1)
    dk[near] = dk1[near] + gback[0].astype(f32)
    dk[few] += jnp.concatenate(keys_back, 1)
    dqt[:, near] += dq1t[...]
    gq = dqt[...].T
    gq = jnp.concatenate([gq[:FAR] + jnp.concatenate(asks_back, 1), gq[FAR:]], 0)
    gq = (gq * SHARP).astype(bf16)
    gv = dv[...].astype(bf16)
    back = dot_nt(gq, uq) + dot_nt(gv, uv)
    back_both = jnp.concatenate(halves(back), 1)
    bu, bl = halves(back.T[: 2 * R])
    lu, ll = halves(lift_s[...])
    from_back = dot(jnp.concatenate([bu, bl], 0), normed_s[...])
    from_back = 2.0 * (from_back[:16] + from_back[16:])
    lifts = jnp.concatenate([lu, ll], 0)
    from_q = dot(lifts, gq)
    from_q = 2.0 * (from_q[:R] + from_q[16 : 16 + R])
    from_v = dot(lifts, gv)
    from_v = 2.0 * (from_v[R:16] + from_v[16 + R : 32])
    pairs = [
        jnp.concatenate([from_back[:R], from_q], 0), jnp.concatenate([from_back[R:16], from_v], 0)
    ]
    for p in range(2):
        for c in range(6):
            part[p * 6 + c] = pairs[p][:, 128 * c : 128 * c + 128].astype(bf16)

    def first(j, carry):
        there = (mine + j) % 16

        @pl.when(there < SLICES)
        def _():
            remote_to(part.at[there], one.at[mine], s_6, r_6, near_peer(j)).start()

        return carry

    lax.fori_loop(1, 16, first, 0)

    @pl.when(mine < SLICES)
    def _():
        pltpu.make_async_copy(part.at[mine], one.at[mine], r_6).start()

    lax.fori_loop(0, GROUPS, keys0, 0)

    @pl.when(mine < SLICES)
    def _():
        drain(one, r_6)
        total[0] = jnp.sum(one[...].astype(f32), 0).astype(bf16)

        def second(j, carry):
            remote_to(total.at[0], two.at[plane], s_7, r_7, across_peer(j)).start()
            return carry

        lax.fori_loop(1, 16, second, 0)
        pltpu.make_async_copy(total.at[0], two.at[plane], r_7).start()

    gk = (dk[...] * LN2).astype(bf16)
    grad = (
        dot_nt(gq, wq_ref[...])
        + dot_nt(gk, wk_ref[...])
        + dot_nt(gv, wv_ref[...])
        + 2.0 * dot(back_both, jnp.concatenate([down, down], 0))
    )
    s = grad * gain_ref[...].astype(f32)

    @pl.when(mine < SLICES)
    def _():
        drain(two, r_7)
        both_sum = jnp.sum(two[...].astype(f32), 0) * (1.0 / math.sqrt(SEQ * DP * T))
        total[1] = both_sum.astype(bf16)

        def third(j, carry):
            remote_to(total.at[1], done.at[mine], s_8, r_8, near_peer(j)).start()
            return carry

        lax.fori_loop(1, 16, third, 0)
        pltpu.make_async_copy(total.at[1], done.at[mine], r_8).start()

    xhat = xhat_s[...]
    out = scale_s[:, 0:1] * (
        s - jnp.mean(s, -1, keepdims=True) - xhat * jnp.mean(s * xhat, -1, keepdims=True)
    )
    row = iota((T, T), 0)
    col = iota((T, T), 1)
    unorder = jnp.where(place_of(col) == row, 1.0, 0.0).astype(bf16)
    out_ref[0] = dot(unorder, out.astype(bf16)).astype(bf16)

    drain(done, r_8)
    for p in range(2):
        for c in range(6):
            tile = done[p * 6 + c].astype(f32)
            merged_ref[2 * p, :, 128 * c : 128 * c + 128] = tile[:R]
            merged_ref[2 * p + 1, :, 128 * c : 128 * c + 128] = tile[R:]

    drain(kv.at[pl.ds(0, (SEQ - 1) * FAR)], s_kv)
    drain(qda.at[pl.ds(0, (CHIPS - 1) * FAR)], s_qd)
    drain(recv2.at[pl.ds(0, (CHIPS - 1) * FAR)], s_2)
    drain(recv3.at[pl.ds(0, (CHIPS - 1) * FAR)], s_3)
    drain(rkvg.at[pl.ds(0, (SEQ - 1) * FAR)], s_4)
    drain(rdq.at[pl.ds(0, (CHIPS - 1) * FAR)], s_5)

    @pl.when(mine < SLICES)
    def _():
        drain(one.at[pl.ds(0, SLICES - 1)], s_6)
        drain(two.at[pl.ds(0, 15)], s_7)
        drain(one.at[pl.ds(0, 15)], s_8)

    @pl.when(mine >= SLICES)
    def _():
        drain(one.at[pl.ds(0, SLICES)], s_6)


def shape(*dims, kind=bf16):
    return jax.ShapeDtypeStruct(dims, kind)


def whole():
    return pl.BlockSpec(memory_space=pltpu.VMEM)


def per_device(
    tiles, cotangent, gain, query_matrix, key_matrix, value_matrix, w_out,
    query_down_factor, query_up_factor, value_down_factor, value_up_factor, valid_count,
):
    buf = pltpu.VMEM
    sem = pltpu.SemaphoreType.DMA
    return pl.pallas_call(
        layer_kernel,
        out_shape=[shape(1, T, D), shape(4, R, D, kind=f32)],
        in_specs=[pl.BlockSpec(memory_space=pltpu.SMEM)] + [whole()] * 11,
        out_specs=[whole()] * 2,
        scratch_shapes=[
            buf((T, D), f32), buf((T, 128), f32), buf((T, D), bf16), buf((2 * R, T), f32),
            buf((T, D), bf16), buf((T, D), bf16), buf((T, D), bf16),
            buf((D, T), bf16), buf((D, T), bf16), buf((D, T), bf16), buf((D, T), bf16),
            buf((H, FAR, 128), bf16), buf((H, FAR, 128), bf16),
            buf((H, T, T), bf16), buf((H, 256, PAIR), bf16),
            buf((T, T), bf16), buf((256, PAIR), bf16),
            buf((H, T), f32), buf((D, T), f32), buf((H, T), f32),
            buf((D, T), bf16), buf((T, D), bf16), buf((D, T), f32), buf((D, PAIR), f32),
            buf((T, D), f32), buf((T, D), f32),
            buf((256, D), bf16), buf((256, D), bf16), buf((D, 256), bf16), buf((D, 256), bf16),
            buf((256, D), f32), buf((256, D), f32),
            buf((2, PAIR, D), bf16), buf((2, PAIR, D), bf16),
            buf((T, 128), bf16), buf((256, 128), bf16), buf((256, T), bf16),
            buf((256, 128), f32), buf((256, 128), f32),
            buf((FAR, 128), f32), buf((256, 128), f32),
            buf((T, 128), bf16), buf((256, 128), bf16), buf((T, 128), bf16), buf((256, 128), bf16),
            buf((SLICES, 16, 128), bf16), buf((16, 16, 128), bf16), buf((2, 16, 128), bf16),
            buf((16, 16, 128), bf16), buf((SLICES, 16, 128), bf16),
            sem, sem, sem, sem, sem((4,)), sem((4,)), sem, sem, sem, sem, sem, sem, sem, sem,
            sem, sem, sem, sem, sem, sem, sem, sem,
        ],
        compiler_params=pltpu.CompilerParams(
            vmem_limit_bytes=VMEM_LIMIT, collective_id=0, has_side_effects=True
        ),
        name="layer",
    )(
        valid_count, tiles, cotangent, gain, query_matrix, key_matrix, value_matrix, w_out,
        query_down_factor.T, query_up_factor, value_down_factor.T, value_up_factor,
    )


def solution(mesh):
    placed = (P("dp", "seq", None),) * 2 + (P(),) * 9 + (P("dp"),)
    return jax.shard_map(
        per_device,
        mesh=mesh,
        in_specs=placed,
        out_specs=(P("dp", "seq", None), P()),
        check_vma=False,
    )
```

```python
import math

import jax
import jax.numpy as jnp
from jax import lax
from jax.experimental import pallas as pl
from jax.experimental.pallas import tpu as pltpu
from jax.sharding import PartitionSpec as P

T = 512
D = 768
H = 16
W = 48
R = 8
PAIR = 128
FAR = 16
SEQ = 32
DP = 8
CHIPS = 16
GROUPS = 2
SLICES = 12
PER = 8
EPS = 1e-5
LOG2E = math.log2(math.e)
SHARP = 1.0 / math.sqrt(W)
LN2 = math.log(2.0)
MESH = pl.DeviceIdType.MESH
f32 = jnp.float32
bf16 = jnp.bfloat16
VMEM_LIMIT = 56 * 1024 * 1024


def iota(shape, axis):
    return lax.broadcasted_iota(jnp.int32, shape, axis)


def dot(a, b):
    return jnp.dot(a, b, preferred_element_type=f32)


def dot_nt(a, b):
    return lax.dot_general(a, b, (((1,), (1,)), ((), ())), preferred_element_type=f32)


def place_of(row):
    return (row & 15) * 32 + ((row >> 4) & 7) * 4 + (row >> 7)


def order_matrix():
    place = place_of(iota((T, 128), 0))
    lane = iota((T, 128), 1)
    parts = [jnp.where(place == lane + 128 * c, 1.0, 0.0) for c in range(4)]
    return jnp.concatenate(parts, 1).astype(bf16)


def halves(value):
    upper = value.astype(bf16)
    lower = (value - upper.astype(f32)).astype(bf16)
    return upper, lower


def normalize(x):
    center = x - jnp.mean(x, -1, keepdims=True)
    inverse = lax.rsqrt(jnp.mean(center * center, -1, keepdims=True) + EPS)
    return center * inverse, inverse


def window(hh):
    low = W * hh
    first = low // 128
    last = (low + W - 1) // 128
    return first * 128, (last - first + 1) * 128, low - first * 128


def pair_window(p):
    low = 2 * W * p
    first = low // 128
    last = (low + 2 * W - 1) // 128
    return first * 128, (last - first + 1) * 128, low - first * 128


def lane_mask(width, off):
    lane = iota((1, width), 1)
    return jnp.where((lane >= off) & (lane < off + W), 1.0, 0.0).astype(bf16)


def pad_rows(block, off, width):
    parts = []
    if off:
        parts.append(jnp.zeros((off, block.shape[1]), block.dtype))
    parts.append(block)
    rest = width - off - block.shape[0]
    if rest:
        parts.append(jnp.zeros((rest, block.shape[1]), block.dtype))
    return jnp.concatenate(parts, 0)


def down_rows(qd_ref, vd_ref):
    return jnp.concatenate(
        [qd_ref[...].astype(f32), vd_ref[...].astype(f32), jnp.zeros((112, D), f32)], 0
    ).astype(bf16)


def up_padded(u_ref, at):
    return pad_rows(u_ref[...].astype(f32), at, 128).astype(bf16)


def layer_kernel(
    valid_ref, tiles_ref, cot_hbm, gain_ref, wq_hbm, wk_hbm, wv_hbm, wo_hbm,
    qd_ref, qu_ref, vd_ref, vu_ref,
    out_ref, done,
    cot_ref, wq_ref, wk_ref, wv_ref, wo_ref, s_in,
    xhat_s, scale_s, normed_s, lift_s, q_ref, k_ref, v_ref, qt_ref, kt_ref, vt_ref, dat_ref,
    sfar,
    e0, e1, mask0, mask1, tot, mix, dlt, dapt, dap, dqt, dq1t, dk, dv,
    k1, v1, k1t, v1t, dk1, dv1, gsend, gback,
    same, other, kv, qda, fe, send2, recv2, send3, recv3, bsame, bother, rsame, rother,
    part, one, total, two,
    s_kv, r_kv, s_qd, r_qd, s_pair, r_pair, s_2, r_2, s_3, r_3, s_4, r_4, s_5, r_5, s_g, r_g,
    s_6, r_6, s_7, r_7, s_8, r_8,
):
    dp = lax.axis_index("dp")
    me = lax.axis_index("seq")
    chip = lax.div(me, 2)
    core = lax.rem(me, 2)
    mate = chip * 2 + (1 - core)
    mine = lax.rem(me, 16)
    half = lax.div(me, 16)
    plane = dp * 2 + half
    valid = valid_ref[0]

    def near_peer(j):
        return {"seq": half * 16 + lax.rem(mine + j, 16)}

    def across_peer(j):
        other = lax.rem(plane + j, 16)
        return {"dp": lax.div(other, 2), "seq": lax.rem(other, 2) * 16 + mine}

    barrier = pltpu.get_barrier_semaphore()

    for j in range(1, SEQ):
        pl.semaphore_signal(
            barrier, inc=1, device_id={"seq": lax.rem(me + j, SEQ)}, device_id_type=MESH
        )
    for j in range(1, 16):
        pl.semaphore_signal(barrier, inc=1, device_id=across_peer(j), device_id_type=MESH)

    def remote_to(src, dst, send, recv, peer):
        return pltpu.make_async_remote_copy(
            src_ref=src, dst_ref=dst, send_sem=send, recv_sem=recv,
            device_id=peer, device_id_type=MESH,
        )

    def remote(src, dst, send, recv, peer):
        return remote_to(src, dst, send, recv, {"seq": peer})

    def drain(ref, sem):
        pltpu.make_async_copy(ref, ref, sem).wait()

    loads = [
        pltpu.make_async_copy(src, dst, s_in.at[i])
        for i, (src, dst) in enumerate(
            [(wq_hbm, wq_ref), (wk_hbm, wk_ref), (wv_hbm, wv_ref), (cot_hbm, cot_ref), (wo_hbm, wo_ref)]
        )
    ]
    for load in loads:
        load.start()

    order = order_matrix()
    x = dot(order, tiles_ref[0])
    xhat, inverse_dev = normalize(x)
    xhat_s[...] = xhat
    scale_s[...] = jnp.broadcast_to(inverse_dev, (T, 128))
    normed = (xhat * gain_ref[...].astype(f32)).astype(bf16)
    normed_s[...] = normed
    down = down_rows(qd_ref, vd_ref)
    uq = up_padded(qu_ref, 0)
    uv = up_padded(vu_ref, R)
    lift = dot_nt(normed, down)
    both = jnp.concatenate(halves(lift), 1)
    lift_s[...] = lift.T[: 2 * R]
    loads[0].wait()
    q = dot(normed, wq_ref[...]) + 2.0 * dot(both, jnp.concatenate([uq, uq], 0))
    q = (q * (SHARP * LOG2E)).astype(bf16)
    q_ref[...] = q
    qt_ref[...] = q.T
    loads[1].wait()
    k = dot(normed, wk_ref[...]).astype(bf16)
    k_ref[...] = k
    kt_ref[...] = k.T
    loads[2].wait()
    v = (dot(normed, wv_ref[...]) + 2.0 * dot(both, jnp.concatenate([uv, uv], 0))).astype(bf16)
    v_ref[...] = v
    vt_ref[...] = v.T
    loads[3].wait()
    loads[4].wait()
    cot = dot(order, cot_ref[0]).astype(bf16)
    da = dot_nt(cot, wo_ref[...]).astype(bf16)
    dat_ref[...] = da.T
    gap = jnp.zeros((FAR, 64 - W), f32)
    qf, kf, vf, df = (rows[:FAR].astype(f32) for rows in (q, k, v, da))
    for h in range(H):
        cut = slice(W * h, W * h + W)
        four = [kf[:, cut], gap, vf[:, cut], gap, qf[:, cut], gap, df[:, cut], gap]
        sfar[h] = jnp.concatenate(four, 1).astype(bf16)

    pl.semaphore_wait(barrier, SEQ - 1 + 15)

    def slot(c):
        return pl.ds(pl.multiple_of(c * FAR, FAR), FAR)

    def around(j):
        return lax.rem(chip + j, CHIPS)

    for j in range(CHIPS):
        there = around(j)
        if j:
            remote(sfar.at[there], same.at[slot(chip)], s_kv, r_kv, there * 2 + core).start()
        keys_only = sfar.at[there, :, pl.ds(0, 128)]
        remote(keys_only, other.at[slot(chip)], s_qd, r_qd, there * 2 + (1 - core)).start()
    pltpu.make_async_copy(sfar.at[chip], same.at[slot(chip)], r_kv).start()

    near = pl.ds(0, PAIR)
    pair_copies = [
        remote(k_ref.at[near], k1, s_pair.at[0], r_pair.at[0], mate),
        remote(v_ref.at[near], v1, s_pair.at[1], r_pair.at[1], mate),
        remote(kt_ref.at[:, near], k1t, s_pair.at[2], r_pair.at[2], mate),
        remote(vt_ref.at[:, near], v1t, s_pair.at[3], r_pair.at[3], mate),
    ]
    for copy in pair_copies:
        copy.start()

    row = iota((T, 128), 0)
    col = iota((T, 128), 1)
    seen = me * T + place_of(row) < valid
    for c in range(4):
        open0 = seen | (row == col + 128 * c)
        mask0[:, 128 * c : 128 * c + 128] = jnp.where(open0, jnp.inf, 0.0).astype(bf16)
    row = iota((PAIR, 2 * PAIR), 0)
    mask1[...] = jnp.where(mate * T + place_of(row) < valid, jnp.inf, 0.0).astype(bf16)
    dk[...] = jnp.zeros_like(dk)
    dv[...] = jnp.zeros_like(dv)
    dk1[...] = jnp.zeros_like(dk1)
    dv1[...] = jnp.zeros_like(dv1)

    def place(g, hh):
        base, width, off = window(hh)
        lanes = pl.ds(pl.multiple_of(g * 384 + base, 128), width)
        rows = pl.ds(pl.multiple_of(g * 384 + W * hh, 16), W)
        return lanes, rows, width, off

    def eight(g):
        return pl.ds(pl.multiple_of(g * PER, PER), PER)

    def forward0(g):
        totals = []
        for hh in range(PER):
            lanes, rows, width, off = place(g, hh)
            ask = pad_rows(qt_ref[rows, :], off, width)
            expo = jnp.exp2(dot(k_ref[:, lanes], ask)).astype(bf16)
            expo = jnp.minimum(expo, mask0[...])
            corner = expo[:PAIR, :PAIR]
            upper = jnp.concatenate([corner + corner, expo[:PAIR, PAIR:]], 1)
            expo = jnp.concatenate([upper, expo[PAIR:]], 0)
            e0[g * PER + hh] = expo
            value = jnp.concatenate([vt_ref[rows, :], jnp.ones((16, T), bf16)], 0)
            mixed = dot(value, expo)
            totals.append(mixed[W : W + 1])
            mix[rows, :] = mixed[:W]
        tot[eight(g), :] = jnp.concatenate(totals, 0)

    def pair_place(g, p):
        base, width, off = pair_window(p)
        lanes = pl.ds(pl.multiple_of(g * 384 + base, 128), width)
        low = pl.ds(pl.multiple_of(g * 384 + 2 * W * p, 16), W)
        high = pl.ds(pl.multiple_of(g * 384 + 2 * W * p + W, 16), W)
        both = pl.ds(pl.multiple_of(g * 384 + 2 * W * p, 16), 2 * W)
        return lanes, low, high, both, width, off

    def side_by_side(low, high, off, width):
        none = jnp.zeros((W, PAIR), bf16)
        block = jnp.concatenate(
            [jnp.concatenate([low, none], 1), jnp.concatenate([none, high], 1)], 0
        )
        return pad_rows(block, off, width)

    def stacked(rows, off, width):
        return jnp.concatenate([rows * lane_mask(width, off), rows * lane_mask(width, off + W)], 0)

    def forward1(g):
        totals = []
        for p in range(PER // 2):
            lanes, low, high, both, width, off = pair_place(g, p)
            ask = side_by_side(qt_ref[low, near], qt_ref[high, near], off, width)
            expo = jnp.exp2(dot(k1[:, lanes], ask)).astype(bf16)
            expo = jnp.minimum(expo, mask1[...])
            e1[g * (PER // 2) + p] = expo
            value = jnp.concatenate([v1t[both, :], jnp.ones((16, PAIR), bf16)], 0)
            mixed = dot(value, expo)
            mix[low, near] += mixed[:W, :PAIR]
            mix[high, near] += mixed[W : 2 * W, PAIR:]
            totals.append(mixed[2 * W : 2 * W + 1, :PAIR])
            totals.append(mixed[2 * W : 2 * W + 1, PAIR:])
        tot[eight(g), near] += jnp.concatenate(totals, 0)

    for g in range(1):
        forward0(g)

    drain(same, r_kv)
    drain(other, r_qd)
    kv[pl.ds(0, 256)] = same[:, :128]
    kv[pl.ds(256, 256)] = other[...]
    qda[...] = same[:, 128:]
    lane = iota((1, 128), 1)
    low = jnp.where(lane < 64, 1.0, 0.0).astype(bf16)
    high = jnp.where(lane >= 64, 1.0, 0.0).astype(bf16)
    i2 = iota((256, T), 0)
    j2 = iota((1, T), 1)
    j2_core = (j2 >> 8) * (1 - core) + (1 - (j2 >> 8)) * core
    j2_pos = (((j2 & 255) >> 4) * 2 + j2_core) * T + (j2 & 15) * 32
    open2 = (j2_pos < valid) | (j2 == i2)
    far_expo = jnp.exp2(dot_nt(qda[...], kv[...] * low))
    far_expo = jnp.where(open2, far_expo, 0.0).astype(bf16)
    fe[...] = far_expo
    first_lane = jnp.where(lane == 0, 1.0, 0.0).astype(bf16)
    far_mixed = dot(far_expo, kv[...] * high + first_lane)
    far_r = jnp.sum(
        jnp.where(lane >= 64, qda[...].astype(f32) * far_mixed, 0.0), 1, keepdims=True
    )
    far_t = far_mixed[:, 0:1]
    send2[...] = jnp.where(lane == chip, far_t, 0.0) + jnp.where(lane == 64 + chip, far_r, 0.0)

    for j in range(1, CHIPS):
        there = around(j)
        remote(send2.at[slot(there)], recv2.at[slot(chip)], s_2, r_2, there * 2 + core).start()
    pltpu.make_async_copy(send2.at[slot(chip)], recv2.at[slot(chip)], r_2).start()

    forward0(1)
    for copy in pair_copies:
        copy.wait()
    for g in range(GROUPS):
        forward1(g)

    drain(recv2, r_2)
    gathered = recv2[pl.ds(0, FAR)]
    for c in range(1, CHIPS):
        gathered = gathered + recv2[pl.ds(c * FAR, FAR)]
    turned = jnp.concatenate([gathered, jnp.zeros((PAIR - FAR, 128), f32)], 0).T
    tot[:, near] += turned[:H]
    inverse = 1.0 / tot[...]
    tot[...] = inverse
    far_sums = jnp.concatenate([turned[64 : 64 + H], jnp.zeros((H, T - PAIR), f32)], 1)
    dlt[...] = far_sums * inverse * inverse
    for h in range(H):
        rows = pl.ds(W * h, W)
        this = tot[h : h + 1, :]
        scaled = (dat_ref[rows, :].astype(f32) * this).astype(bf16)
        dapt[rows, :] = scaled
        own = jnp.sum(scaled.astype(f32) * mix[rows, :], 0, keepdims=True)
        dlt[h : h + 1, :] += own * this
    filler = jnp.zeros((64 - H, 128), f32)
    send3[...] = jnp.concatenate([tot[:, near], filler, dlt[:, near], filler], 0).T[:FAR]

    for j in range(1, CHIPS):
        there = around(j)
        remote(send3, recv3.at[slot(chip)], s_3, r_3, there * 2 + core).start()
    pltpu.make_async_copy(send3, recv3.at[slot(chip)], r_3).start()
    dap[...] = dapt[...].T

    def backward0(g):
        deltas = dlt[eight(g), :]
        for hh in range(PER):
            lanes, rows, width, off = place(g, hh)
            expo = e0[g * PER + hh]
            dprob = dot(v_ref[:, lanes], pad_rows(dapt[rows, :], off, width))
            dscore = expo * (dprob - deltas[hh : hh + 1]).astype(bf16)
            e0[g * PER + hh] = dscore
            dqt[rows, :] = dot(kt_ref[rows, :], dscore)
            dv[:, lanes] += dot(expo, dap[:, lanes] * lane_mask(width, off))

    def backward1(g):
        deltas = dlt[eight(g), near]
        for p in range(PER // 2):
            lanes, low, high, both, width, off = pair_place(g, p)
            expo = e1[g * (PER // 2) + p]
            dprob = dot(v1[:, lanes], side_by_side(dapt[low, near], dapt[high, near], off, width))
            delta = jnp.concatenate([deltas[2 * p : 2 * p + 1], deltas[2 * p + 1 : 2 * p + 2]], 1)
            dscore = expo * (dprob - delta).astype(bf16)
            dq = dot(k1t[both, :], dscore)
            dq1t[low, :] = dq[:W, :PAIR]
            dq1t[high, :] = dq[W:, PAIR:]
            dv1[:, lanes] += dot(expo, stacked(dap[near, lanes], off, width))
            dk1[:, lanes] += dot(dscore, stacked(q_ref[near, lanes], off, width))

    def keys0(g):
        for hh in range(PER):
            lanes, rows, width, off = place(g, hh)
            dk[:, lanes] += dot(e0[g * PER + hh], q_ref[:, lanes] * lane_mask(width, off))

    for g in range(GROUPS):
        backward1(g)
    gsend[0] = dk1[...].astype(bf16)
    gsend[1] = dv1[...].astype(bf16)
    grad_copy = remote(gsend, gback, s_g, r_g, mate)
    grad_copy.start()
    backward0(0)

    drain(recv3, r_3)
    scales = recv3[...]
    far_inv = jnp.sum(jnp.where(lane == chip, scales, 0.0), 1, keepdims=True)
    far_del = jnp.sum(jnp.where(lane == 64 + chip, scales, 0.0), 1, keepdims=True)
    far_grads = jnp.where(lane >= 64, qda[...].astype(f32) * far_inv, 0.0).astype(bf16)
    far_back = fe[...].astype(f32)
    far_ds = far_back * (dot_nt(far_grads, kv[...] * high) - far_del)
    back_kv = (
        dot(far_ds.T.astype(bf16), qda[...] * low) + dot(far_back.T.astype(bf16), far_grads)
    ).astype(bf16)
    bsame[:, :128] = back_kv[:256]
    bsame[:, 128:] = dot(far_ds.astype(bf16), kv[...] * low).astype(bf16)
    bother[...] = back_kv[256:]
    for j in range(CHIPS):
        there = around(j)
        if j:
            remote(
                bsame.at[slot(there)], rsame.at[slot(chip)], s_4, r_4, there * 2 + core
            ).start()
        remote(
            bother.at[slot(there)], rother.at[slot(chip)], s_5, r_5, there * 2 + (1 - core)
        ).start()
    pltpu.make_async_copy(bsame.at[slot(chip)], rsame.at[slot(chip)], r_4).start()

    backward0(1)

    grad_copy.wait()
    drain(rsame, r_4)
    drain(rother, r_5)
    keys_back, values_back, asks_back = [], [], []
    for h in range(H):
        both_back = rsame[pl.ds(h * FAR, FAR)].astype(f32)
        here = both_back[:, :128] + rother[pl.ds(h * FAR, FAR)].astype(f32)
        keys_back.append(here[:, :W])
        values_back.append(here[:, 64 : 64 + W])
        asks_back.append(both_back[:, 128 : 128 + W])
    few = pl.ds(0, FAR)
    dv[near] += gback[1].astype(f32)
    dv[few] += jnp.concatenate(values_back, 1)
    dk[near] = gback[0].astype(f32)
    dk[few] += jnp.concatenate(keys_back, 1)
    dqt[:, near] += dq1t[...]
    gq = dqt[...].T
    gq = jnp.concatenate([gq[:FAR] + jnp.concatenate(asks_back, 1), gq[FAR:]], 0)
    gq = (gq * SHARP).astype(bf16)
    gv = dv[...].astype(bf16)
    back = dot_nt(gq, uq) + dot_nt(gv, uv)
    back_both = jnp.concatenate(halves(back), 1)
    bu, bl = halves(back.T[: 2 * R])
    lu, ll = halves(lift_s[...])
    from_back = dot(jnp.concatenate([bu, bl], 0), normed_s[...])
    from_back = 2.0 * (from_back[:16] + from_back[16:])
    lifts = jnp.concatenate([lu, ll], 0)
    from_q = dot(lifts, gq)
    from_q = 2.0 * (from_q[:R] + from_q[16 : 16 + R])
    from_v = dot(lifts, gv)
    from_v = 2.0 * (from_v[R:16] + from_v[16 + R : 32])
    pairs = [
        jnp.concatenate([from_back[:R], from_q], 0), jnp.concatenate([from_back[R:16], from_v], 0)
    ]
    for p in range(2):
        for c in range(6):
            part[p * 6 + c] = pairs[p][:, 128 * c : 128 * c + 128].astype(bf16)

    def first(j, carry):
        there = lax.rem(mine + j, 16)

        @pl.when(there < SLICES)
        def _():
            remote_to(part.at[there], one.at[mine], s_6, r_6, near_peer(j)).start()

        return carry

    lax.fori_loop(1, 16, first, 0)

    @pl.when(mine < SLICES)
    def _():
        pltpu.make_async_copy(part.at[mine], one.at[mine], r_6).start()

    for g in range(GROUPS):
        keys0(g)

    @pl.when(mine < SLICES)
    def _():
        drain(one, r_6)
        total[0] = jnp.sum(one[...].astype(f32), 0).astype(bf16)

        for j in range(1, 16):
            remote_to(total.at[0], two.at[plane], s_7, r_7, across_peer(j)).start()
        pltpu.make_async_copy(total.at[0], two.at[plane], r_7).start()

    gk = (dk[...] * LN2).astype(bf16)
    grad = (
        dot_nt(gq, wq_ref[...])
        + dot_nt(gk, wk_ref[...])
        + dot_nt(gv, wv_ref[...])
        + 2.0 * dot(back_both, jnp.concatenate([down, down], 0))
    )
    s = grad * gain_ref[...].astype(f32)

    @pl.when(mine < SLICES)
    def _():
        drain(two, r_7)
        both_sum = jnp.sum(two[...].astype(f32), 0) * (1.0 / math.sqrt(SEQ * DP * T))
        total[1] = both_sum.astype(bf16)

        for j in range(1, 16):
            remote_to(total.at[1], done.at[mine], s_8, r_8, near_peer(j)).start()
        pltpu.make_async_copy(total.at[1], done.at[mine], r_8).start()

    xhat = xhat_s[...]
    out = scale_s[:, 0:1] * (
        s - jnp.mean(s, -1, keepdims=True) - xhat * jnp.mean(s * xhat, -1, keepdims=True)
    )
    out_ref[...] = out.astype(bf16)
    drain(done, r_8)

    drain(same.at[pl.ds(0, (CHIPS - 1) * FAR)], s_kv)
    drain(other, s_qd)
    drain(recv2.at[pl.ds(0, (CHIPS - 1) * FAR)], s_2)
    drain(recv3.at[pl.ds(0, (CHIPS - 1) * FAR)], s_3)
    drain(rsame.at[pl.ds(0, (CHIPS - 1) * FAR)], s_4)
    drain(rother, s_5)

    @pl.when(mine < SLICES)
    def _():
        drain(one.at[pl.ds(0, SLICES - 1)], s_6)
        drain(two.at[pl.ds(0, 15)], s_7)
        drain(one.at[pl.ds(0, 15)], s_8)

    @pl.when(mine >= SLICES)
    def _():
        drain(one.at[pl.ds(0, SLICES)], s_6)


def place_kernel(y_ref, done_ref, out_ref, merged_ref):
    unorder = jnp.where(place_of(iota((1, T), 1)) == iota((T, T), 0), 1.0, 0.0).astype(bf16)
    out_ref[0] = dot(unorder, y_ref[...]).astype(bf16)
    for p in range(2):
        for c in range(6):
            tile = done_ref[p * 6 + c].astype(f32)
            merged_ref[2 * p, :, 128 * c : 128 * c + 128] = tile[:R]
            merged_ref[2 * p + 1, :, 128 * c : 128 * c + 128] = tile[R:]


def shape(*dims, kind=bf16):
    return jax.ShapeDtypeStruct(dims, kind)


def whole():
    return pl.BlockSpec(memory_space=pltpu.VMEM)


def far():
    return pl.BlockSpec(memory_space=pl.ANY)


def per_device(
    tiles, cotangent, gain, query_matrix, key_matrix, value_matrix, w_out,
    query_down_factor, query_up_factor, value_down_factor, value_up_factor, valid_count,
):
    buf = pltpu.VMEM
    sem = pltpu.SemaphoreType.DMA
    y, done = pl.pallas_call(
        layer_kernel,
        out_shape=[shape(T, D), shape(SLICES, 16, 128)],
        in_specs=[pl.BlockSpec(memory_space=pltpu.SMEM), whole(), far(), whole()] + [far()] * 4
        + [whole()] * 4,
        out_specs=[whole()] * 2,
        scratch_shapes=[
            buf((1, T, D), bf16), buf((D, D), bf16), buf((D, D), bf16), buf((D, D), bf16),
            buf((D, D), bf16), sem((5,)),
            buf((T, D), f32), buf((T, 128), f32), buf((T, D), bf16), buf((2 * R, T), f32),
            buf((T, D), bf16), buf((T, D), bf16), buf((T, D), bf16),
            buf((D, T), bf16), buf((D, T), bf16), buf((D, T), bf16), buf((D, T), bf16),
            buf((H, FAR, 256), bf16),
            buf((H, T, T), bf16), buf((H // 2, PAIR, 256), bf16),
            buf((T, T), bf16), buf((PAIR, 256), bf16),
            buf((H, T), f32), buf((D, T), f32), buf((H, T), f32),
            buf((D, T), bf16), buf((T, D), bf16), buf((D, T), f32), buf((D, PAIR), f32),
            buf((T, D), f32), buf((T, D), f32),
            buf((PAIR, D), bf16), buf((PAIR, D), bf16), buf((D, PAIR), bf16), buf((D, PAIR), bf16),
            buf((PAIR, D), f32), buf((PAIR, D), f32),
            buf((2, PAIR, D), bf16), buf((2, PAIR, D), bf16),
            buf((256, 256), bf16), buf((256, 128), bf16),
            buf((T, 128), bf16), buf((256, 128), bf16), buf((256, T), bf16),
            buf((256, 128), f32), buf((256, 128), f32),
            buf((FAR, 128), f32), buf((256, 128), f32),
            buf((256, 256), bf16), buf((256, 128), bf16),
            buf((256, 256), bf16), buf((256, 128), bf16),
            buf((SLICES, 16, 128), bf16), buf((16, 16, 128), bf16), buf((2, 16, 128), bf16),
            buf((16, 16, 128), bf16),
            sem, sem, sem, sem, sem((4,)), sem((4,)), sem, sem, sem, sem, sem, sem, sem, sem,
            sem, sem, sem, sem, sem, sem, sem, sem,
        ],
        compiler_params=pltpu.CompilerParams(
            vmem_limit_bytes=VMEM_LIMIT, collective_id=0, has_side_effects=True
        ),
        name="layer",
    )(
        valid_count, tiles, cotangent, gain, query_matrix, key_matrix, value_matrix, w_out,
        query_down_factor.T, query_up_factor, value_down_factor.T, value_up_factor,
    )
    return pl.pallas_call(
        place_kernel,
        out_shape=[shape(1, T, D), shape(4, R, D, kind=f32)],
        in_specs=[whole()] * 2,
        out_specs=[whole()] * 2,
        name="place",
    )(y, done)


def solution(mesh):
    placed = (P("dp", "seq", None),) * 2 + (P(),) * 9 + (P("dp"),)
    return jax.shard_map(
        per_device,
        mesh=mesh,
        in_specs=placed,
        out_specs=(P("dp", "seq", None), P()),
        check_vma=False,
    )
```

```python
import math

import jax
import jax.numpy as jnp
from jax import lax
from jax.experimental import pallas as pl
from jax.experimental.pallas import tpu as pltpu
from jax.sharding import PartitionSpec as P

T = 512
D = 768
H = 16
W = 48
R = 8
PAIR = 128
FAR = 16
SEQ = 32
DP = 8
CHIPS = 16
GROUPS = 2
SLICES = 12
PER = 8
EPS = 1e-5
LOG2E = math.log2(math.e)
SHARP = 1.0 / math.sqrt(W)
LN2 = math.log(2.0)
MESH = pl.DeviceIdType.MESH
f32 = jnp.float32
bf16 = jnp.bfloat16
VMEM_LIMIT = 56 * 1024 * 1024


def iota(shape, axis):
    return lax.broadcasted_iota(jnp.int32, shape, axis)


def dot(a, b):
    return jnp.dot(a, b, preferred_element_type=f32)


def dot_nt(a, b):
    return lax.dot_general(a, b, (((1,), (1,)), ((), ())), preferred_element_type=f32)


def place_of(row):
    return (row & 15) * 32 + ((row >> 4) & 7) * 4 + (row >> 7)


def order_matrix():
    place = place_of(iota((T, 128), 0))
    lane = iota((T, 128), 1)
    parts = [jnp.where(place == lane + 128 * c, 1.0, 0.0) for c in range(4)]
    return jnp.concatenate(parts, 1).astype(bf16)


def halves(value):
    upper = value.astype(bf16)
    lower = (value - upper.astype(f32)).astype(bf16)
    return upper, lower


def normalize(x):
    center = x - jnp.mean(x, -1, keepdims=True)
    inverse = lax.rsqrt(jnp.mean(center * center, -1, keepdims=True) + EPS)
    return center * inverse, inverse


def window(hh):
    low = W * hh
    first = low // 128
    last = (low + W - 1) // 128
    return first * 128, (last - first + 1) * 128, low - first * 128


def pair_window(p):
    low = 2 * W * p
    first = low // 128
    last = (low + 2 * W - 1) // 128
    return first * 128, (last - first + 1) * 128, low - first * 128


def lane_mask(width, off):
    lane = iota((1, width), 1)
    return jnp.where((lane >= off) & (lane < off + W), 1.0, 0.0).astype(bf16)


def pad_rows(block, off, width):
    parts = []
    if off:
        parts.append(jnp.zeros((off, block.shape[1]), block.dtype))
    parts.append(block)
    rest = width - off - block.shape[0]
    if rest:
        parts.append(jnp.zeros((rest, block.shape[1]), block.dtype))
    return jnp.concatenate(parts, 0)


def down_rows(qd_ref, vd_ref):
    return jnp.concatenate(
        [qd_ref[...].astype(f32), vd_ref[...].astype(f32), jnp.zeros((112, D), f32)], 0
    ).astype(bf16)


def up_padded(u_ref, at):
    return pad_rows(u_ref[...].astype(f32), at, 128).astype(bf16)


def layer_kernel(
    valid_ref, tiles_ref, cot_hbm, gain_ref, wq_hbm, wk_hbm, wv_hbm, wo_hbm,
    qd_ref, qu_ref, vd_ref, vu_ref,
    out_ref, merged_ref,
    cot_ref, wq_ref, wk_ref, wv_ref, wo_ref, s_in, out_s, s_out,
    xhat_s, scale_s, normed_s, lift_s, q_ref, k_ref, v_ref, qt_ref, kt_ref, dat_ref,
    sfar,
    e0, p0, e1, p1, mask0, mask1, tot, rsum, dlt, dap, dqt, dq1t, dk, dv,
    k1, v1, k1t, dk1, dv1, gsend, gback,
    same, other, kv, qda, fe, send2, recv2, send3, recv3, bsame, bother, rsame, rother,
    part, one, total, two, done,
    s_kv, r_kv, s_qd, r_qd, s_pair, r_pair, s_2, r_2, s_3, r_3, s_4, r_4, s_5, r_5, s_g, r_g,
    s_6, r_6, s_7, r_7, s_8, r_8,
):
    dp = lax.axis_index("dp")
    me = lax.axis_index("seq")
    chip = lax.div(me, 2)
    core = lax.rem(me, 2)
    mate = chip * 2 + (1 - core)
    column = lax.rem(me, 16)
    half = lax.div(me, 16)
    mine = dp * 2 + half
    valid = valid_ref[0]

    def plane_peer(j):
        there = lax.rem(mine + j, 16)
        return {"dp": lax.div(there, 2), "seq": lax.rem(there, 2) * 16 + column}

    def column_peer(j):
        return {"seq": half * 16 + lax.rem(column + j, 16)}

    barrier = pltpu.get_barrier_semaphore()

    for j in range(1, SEQ):
        pl.semaphore_signal(
            barrier, inc=1, device_id={"seq": lax.rem(me + j, SEQ)}, device_id_type=MESH
        )
    for j in range(1, 16):
        pl.semaphore_signal(barrier, inc=1, device_id=plane_peer(j), device_id_type=MESH)

    def remote_to(src, dst, send, recv, peer):
        return pltpu.make_async_remote_copy(
            src_ref=src, dst_ref=dst, send_sem=send, recv_sem=recv,
            device_id=peer, device_id_type=MESH,
        )

    def remote(src, dst, send, recv, peer):
        return remote_to(src, dst, send, recv, {"seq": peer})

    def drain(ref, sem):
        pltpu.make_async_copy(ref, ref, sem).wait()

    loads = [
        pltpu.make_async_copy(src, dst, s_in.at[i])
        for i, (src, dst) in enumerate(
            [(cot_hbm, cot_ref), (wo_hbm, wo_ref), (wq_hbm, wq_ref), (wk_hbm, wk_ref), (wv_hbm, wv_ref)]
        )
    ]
    for load in loads:
        load.start()

    order = order_matrix()
    x = dot(order, tiles_ref[0])
    loads[0].wait()
    loads[1].wait()
    cot = dot(order, cot_ref[0]).astype(bf16)
    da = dot_nt(cot, wo_ref[...]).astype(bf16)
    dat_ref[...] = da.T
    xhat, inverse_dev = normalize(x)
    xhat_s[...] = xhat
    scale_s[...] = jnp.broadcast_to(inverse_dev, (T, 128))
    normed = (xhat * gain_ref[...].astype(f32)).astype(bf16)
    normed_s[...] = normed
    down = down_rows(qd_ref, vd_ref)
    uq = up_padded(qu_ref, 0)
    uv = up_padded(vu_ref, R)
    lift = dot_nt(normed, down)
    both = jnp.concatenate(halves(lift), 1)
    lift_s[...] = lift.T[: 2 * R]
    loads[2].wait()
    loads[3].wait()
    loads[4].wait()
    q = dot(normed, wq_ref[...]) + 2.0 * dot(both, jnp.concatenate([uq, uq], 0))
    q = (q * (SHARP * LOG2E)).astype(bf16)
    q_ref[...] = q
    qt_ref[...] = q.T
    k = dot(normed, wk_ref[...]).astype(bf16)
    k_ref[...] = k
    kt_ref[...] = k.T
    v = (dot(normed, wv_ref[...]) + 2.0 * dot(both, jnp.concatenate([uv, uv], 0))).astype(bf16)
    v_ref[...] = v
    gap = jnp.zeros((FAR, 64 - W), f32)
    qf, kf, vf, df = (rows[:FAR].astype(f32) for rows in (q, k, v, da))
    for h in range(H):
        cut = slice(W * h, W * h + W)
        four = [kf[:, cut], gap, vf[:, cut], gap, qf[:, cut], gap, df[:, cut], gap]
        sfar[h] = jnp.concatenate(four, 1).astype(bf16)

    pl.semaphore_wait(barrier, SEQ - 1 + 15)

    def slot(c):
        return pl.ds(pl.multiple_of(c * FAR, FAR), FAR)

    def around(j):
        return lax.rem(chip + j, CHIPS)

    for j in range(CHIPS):
        there = around(j)
        if j:
            remote(sfar.at[there], same.at[slot(chip)], s_kv, r_kv, there * 2 + core).start()
        keys_only = sfar.at[there, :, pl.ds(0, 128)]
        remote(keys_only, other.at[slot(chip)], s_qd, r_qd, there * 2 + (1 - core)).start()
    pltpu.make_async_copy(sfar.at[chip], same.at[slot(chip)], r_kv).start()

    near = pl.ds(0, PAIR)
    pair_copies = [
        remote(k_ref.at[near], k1, s_pair.at[0], r_pair.at[0], mate),
        remote(v_ref.at[near], v1, s_pair.at[1], r_pair.at[1], mate),
        remote(kt_ref.at[:, near], k1t, s_pair.at[2], r_pair.at[2], mate),
    ]
    for copy in pair_copies:
        copy.start()

    row = iota((T, 128), 0)
    col = iota((T, 128), 1)
    seen = me * T + place_of(row) < valid
    for c in range(4):
        open0 = seen | (row == col + 128 * c)
        mask0[:, 128 * c : 128 * c + 128] = jnp.where(open0, jnp.inf, 0.0).astype(bf16)
    row = iota((PAIR, 2 * PAIR), 0)
    mask1[...] = jnp.where(mate * T + place_of(row) < valid, jnp.inf, 0.0).astype(bf16)

    def place(g, hh):
        base, width, off = window(hh)
        return pl.ds(g * 384 + base, width), pl.ds(g * 384 + W * hh, W), width, off

    def eight(g):
        return pl.ds(pl.multiple_of(g * PER, PER), PER)

    def scores(h):
        lanes, rows, width, off = place(h // PER, h % PER)
        return (
            dot(k_ref[:, lanes], pad_rows(qt_ref[rows, :], off, width)),
            dot(v_ref[:, lanes], pad_rows(dat_ref[rows, :], off, width)),
        )

    def column_sums(expo, dprob):
        expo = expo.astype(f32)
        return jnp.sum(expo, 0, keepdims=True), jnp.sum(expo * dprob, 0, keepdims=True)

    def forward0(heads):
        score, dprob = scores(heads[0])
        for h in heads:
            ahead = scores(h + 1) if h + 1 in heads else (None, None)
            expo = jnp.minimum(jnp.exp2(score).astype(bf16), mask0[...])
            corner = expo[:PAIR, :PAIR]
            upper = jnp.concatenate([corner + corner, expo[:PAIR, PAIR:]], 1)
            expo = jnp.concatenate([upper, expo[PAIR:]], 0)
            e0[h] = expo
            p0[h] = dprob.astype(bf16)
            tot[h : h + 1, :], rsum[h : h + 1, :] = column_sums(expo, dprob)
            score, dprob = ahead

    def pair_place(g, p):
        base, width, off = pair_window(p)
        lanes = pl.ds(g * 384 + base, width)
        low = pl.ds(pl.multiple_of(g * 384 + 2 * W * p, 16), W)
        high = pl.ds(pl.multiple_of(g * 384 + 2 * W * p + W, 16), W)
        both = pl.ds(pl.multiple_of(g * 384 + 2 * W * p, 16), 2 * W)
        return lanes, low, high, both, width, off

    def side_by_side(low, high, off, width):
        none = jnp.zeros((W, PAIR), bf16)
        block = jnp.concatenate(
            [jnp.concatenate([low, none], 1), jnp.concatenate([none, high], 1)], 0
        )
        return pad_rows(block, off, width)

    def stacked(rows, off, width):
        return jnp.concatenate([rows * lane_mask(width, off), rows * lane_mask(width, off + W)], 0)

    def forward1(g):
        totals, sums = [], []
        for p in range(PER // 2):
            lanes, low, high, both, width, off = pair_place(g, p)
            ask = side_by_side(qt_ref[low, near], qt_ref[high, near], off, width)
            given = side_by_side(dat_ref[low, near], dat_ref[high, near], off, width)
            expo = jnp.minimum(jnp.exp2(dot(k1[:, lanes], ask)).astype(bf16), mask1[...])
            dprob = dot(v1[:, lanes], given)
            e1[g * (PER // 2) + p] = expo
            p1[g * (PER // 2) + p] = dprob.astype(bf16)
            here, mixed = column_sums(expo, dprob)
            totals += [here[:, :PAIR], here[:, PAIR:]]
            sums += [mixed[:, :PAIR], mixed[:, PAIR:]]
        tot[eight(g), near] += jnp.concatenate(totals, 0)
        rsum[eight(g), near] += jnp.concatenate(sums, 0)

    forward0(range(0, 10))

    drain(same, r_kv)
    drain(other, r_qd)
    kv[pl.ds(0, 256)] = same[:, :128]
    kv[pl.ds(256, 256)] = other[...]
    qda[...] = same[:, 128:]
    lane = iota((1, 128), 1)
    low = jnp.where(lane < 64, 1.0, 0.0).astype(bf16)
    high = jnp.where(lane >= 64, 1.0, 0.0).astype(bf16)
    i2 = iota((256, T), 0)
    j2 = iota((1, T), 1)
    j2_core = (j2 >> 8) * (1 - core) + (1 - (j2 >> 8)) * core
    j2_pos = (((j2 & 255) >> 4) * 2 + j2_core) * T + (j2 & 15) * 32
    open2 = (j2_pos < valid) | (j2 == i2)
    far_expo = jnp.exp2(dot_nt(qda[...], kv[...] * low))
    far_expo = jnp.where(open2, far_expo, 0.0).astype(bf16)
    fe[...] = far_expo
    first_lane = jnp.where(lane == 0, 1.0, 0.0).astype(bf16)
    far_mixed = dot(far_expo, kv[...] * high + first_lane)
    far_r = jnp.sum(
        jnp.where(lane >= 64, qda[...].astype(f32) * far_mixed, 0.0), 1, keepdims=True
    )
    far_t = far_mixed[:, 0:1]
    far_parts = halves(far_t) + halves(far_r)
    packed = jnp.zeros((256, 128), f32)
    for i in range(4):
        packed = packed + jnp.where(lane == 16 * i + chip, far_parts[i].astype(f32), 0.0)
    send2[...] = packed.astype(bf16)

    for j in range(1, CHIPS):
        there = around(j)
        remote(send2.at[slot(there)], recv2.at[slot(chip)], s_2, r_2, there * 2 + core).start()
    pltpu.make_async_copy(send2.at[slot(chip)], recv2.at[slot(chip)], r_2).start()

    forward0(range(10, 16))
    for copy in pair_copies:
        copy.wait()
    for g in range(GROUPS):
        forward1(g)

    drain(recv2, r_2)
    gathered = recv2[pl.ds(0, FAR)].astype(f32)
    for c in range(1, CHIPS):
        gathered = gathered + recv2[pl.ds(c * FAR, FAR)].astype(f32)
    turned = jnp.concatenate([gathered, jnp.zeros((PAIR - FAR, 128), f32)], 0).T
    tot[:, near] += turned[:16] + turned[16:32]
    inverse = 1.0 / tot[...]
    tot[...] = inverse
    rsum[:, near] += turned[32:48] + turned[48:64]
    dlt[...] = rsum[...] * inverse * inverse
    scale_parts = [part.astype(f32) for part in halves(tot[:, near]) + halves(dlt[:, near])]
    scale_parts.append(jnp.zeros((64, 128), f32))
    send3[...] = jnp.concatenate(scale_parts, 0).T[:FAR].astype(bf16)

    for j in range(1, CHIPS):
        there = around(j)
        remote(send3, recv3.at[slot(chip)], s_3, r_3, there * 2 + core).start()
    pltpu.make_async_copy(send3, recv3.at[slot(chip)], r_3).start()
    scaled = []
    for h in range(H):
        rows = pl.ds(W * h, W)
        scaled.append((dat_ref[rows, :].astype(f32) * tot[h : h + 1, :]).astype(bf16))
    dap[...] = jnp.concatenate(scaled, 0).T

    def gather_in(ref, lanes, width, value, fresh):
        if width == 128:
            if fresh:
                ref[:, lanes] = value
            else:
                ref[:, lanes] += value
        else:
            ref[:, pl.ds(lanes.start, 128)] += value[:, :128]
            ref[:, pl.ds(lanes.start + 128, 128)] = value[:, 128:]

    def dscores(h):
        dprob = p0[h].astype(f32) * tot[h : h + 1, :] - dlt[h : h + 1, :]
        return e0[h] * dprob.astype(bf16)

    def backward0(heads):
        dscore = dscores(heads[0])
        for h in heads:
            lanes, rows, width, off = place(h // PER, h % PER)
            value = dot(e0[h], dap[:, lanes] * lane_mask(width, off))
            gather_in(dv, lanes, width, value, h % PER == 0)
            ahead = dscores(h + 1) if h + 1 in heads else None
            p0[h] = dscore
            dqt[rows, :] = dot(kt_ref[rows, :], dscore)
            dscore = ahead

    def backward1(g):
        for p in range(PER // 2):
            lanes, low, high, both, width, off = pair_place(g, p)
            expo = e1[g * (PER // 2) + p]
            a, b = g * PER + 2 * p, g * PER + 2 * p + 1
            scale = jnp.concatenate([tot[a : a + 1, near], tot[b : b + 1, near]], 1)
            delta = jnp.concatenate([dlt[a : a + 1, near], dlt[b : b + 1, near]], 1)
            dprob = p1[g * (PER // 2) + p].astype(f32) * scale - delta
            dscore = expo * dprob.astype(bf16)
            dq = dot(k1t[both, :], dscore)
            dq1t[low, :] = dq[:W, :PAIR]
            dq1t[high, :] = dq[W:, PAIR:]
            value = dot(expo, stacked(dap[near, lanes], off, width))
            gather_in(dv1, lanes, width, value, p == 0)
            value = dot(dscore, stacked(q_ref[near, lanes], off, width))
            gather_in(dk1, lanes, width, value, p == 0)

    def keys0(g):
        for hh in range(PER):
            lanes, rows, width, off = place(g, hh)
            value = dot(p0[g * PER + hh], q_ref[:, lanes] * lane_mask(width, off))
            gather_in(dk, lanes, width, value, hh == 0)

    for g in range(GROUPS):
        backward1(g)
    gsend[0] = dk1[...].astype(bf16)
    gsend[1] = dv1[...].astype(bf16)
    grad_copy = remote(gsend, gback, s_g, r_g, mate)
    grad_copy.start()
    backward0(range(0, 4))

    drain(recv3, r_3)
    scales = recv3[...].astype(f32)
    for_head = (lane & 15) == chip
    far_inv = jnp.sum(jnp.where(for_head & (lane < 32), scales, 0.0), 1, keepdims=True)
    far_del = jnp.sum(jnp.where(for_head & (lane >= 32), scales, 0.0), 1, keepdims=True)
    far_grads = jnp.where(lane >= 64, qda[...].astype(f32) * far_inv, 0.0).astype(bf16)
    far_back = fe[...].astype(f32)
    far_ds = far_back * (dot_nt(far_grads, kv[...] * high) - far_del)
    back_kv = (
        dot(far_ds.T.astype(bf16), qda[...] * low) + dot(far_back.T.astype(bf16), far_grads)
    ).astype(bf16)
    bsame[:, :128] = back_kv[:256]
    bsame[:, 128:] = dot(far_ds.astype(bf16), kv[...] * low).astype(bf16)
    bother[...] = back_kv[256:]
    for j in range(CHIPS):
        there = around(j)
        if j:
            remote(
                bsame.at[slot(there)], rsame.at[slot(chip)], s_4, r_4, there * 2 + core
            ).start()
        remote(
            bother.at[slot(there)], rother.at[slot(chip)], s_5, r_5, there * 2 + (1 - core)
        ).start()
    pltpu.make_async_copy(bsame.at[slot(chip)], rsame.at[slot(chip)], r_4).start()

    backward0(range(4, 16))

    grad_copy.wait()
    drain(rsame, r_4)
    drain(rother, r_5)
    keys_back, values_back, asks_back = [], [], []
    for h in range(H):
        both_back = rsame[pl.ds(h * FAR, FAR)].astype(f32)
        here = both_back[:, :128] + rother[pl.ds(h * FAR, FAR)].astype(f32)
        keys_back.append(here[:, :W])
        values_back.append(here[:, 64 : 64 + W])
        asks_back.append(both_back[:, 128 : 128 + W])
    few = pl.ds(0, FAR)
    dv[near] += gback[1].astype(f32)
    dv[few] += jnp.concatenate(values_back, 1)
    dqt[:, near] += dq1t[...]
    gq = (dqt[...] * SHARP).astype(bf16).T
    first_rows = dqt[:, near].T[:FAR] + jnp.concatenate(asks_back, 1)
    gq = jnp.concatenate([(first_rows * SHARP).astype(bf16), gq[FAR:]], 0)
    gv = dv[...].astype(bf16)
    back = dot_nt(gq, uq) + dot_nt(gv, uv)
    back_both = jnp.concatenate(halves(back), 1)
    bu, bl = halves(back.T[: 2 * R])
    lu, ll = halves(lift_s[...])
    from_back = dot(jnp.concatenate([bu, bl], 0), normed_s[...])
    from_back = 2.0 * (from_back[:16] + from_back[16:])
    lifts = jnp.concatenate([lu, ll], 0)
    from_q = dot(lifts, gq)
    from_q = 2.0 * (from_q[:R] + from_q[16 : 16 + R])
    from_v = dot(lifts, gv)
    from_v = 2.0 * (from_v[R:16] + from_v[16 + R : 32])
    pairs = [
        jnp.concatenate([from_back[:R], from_q], 0), jnp.concatenate([from_back[R:16], from_v], 0)
    ]
    for p in range(2):
        for c in range(6):
            part[p * 6 + c] = pairs[p][:, 128 * c : 128 * c + 128].astype(bf16)

    def first(j, carry):
        there = lax.rem(mine + j, 16)

        @pl.when(there < SLICES)
        def _():
            remote_to(part.at[there], one.at[mine], s_6, r_6, plane_peer(j)).start()

        return carry

    lax.fori_loop(1, 16, first, 0)

    @pl.when(mine < SLICES)
    def _():
        pltpu.make_async_copy(part.at[mine], one.at[mine], r_6).start()

    for g in range(GROUPS):
        keys0(g)

    @pl.when(mine < SLICES)
    def _():
        drain(one, r_6)
        total[0] = jnp.sum(one[...].astype(f32), 0).astype(bf16)

        for j in range(1, 16):
            remote_to(total.at[0], two.at[column], s_7, r_7, column_peer(j)).start()
        pltpu.make_async_copy(total.at[0], two.at[column], r_7).start()

    dk[near] += gback[0].astype(f32)
    dk[few] += jnp.concatenate(keys_back, 1)
    gk = (dk[...] * LN2).astype(bf16)
    grad = (
        dot_nt(gq, wq_ref[...])
        + dot_nt(gk, wk_ref[...])
        + dot_nt(gv, wv_ref[...])
        + 2.0 * dot(back_both, jnp.concatenate([down, down], 0))
    )
    s = grad * gain_ref[...].astype(f32)

    @pl.when(mine < SLICES)
    def _():
        drain(two, r_7)
        both_sum = jnp.sum(two[...].astype(f32), 0) * (1.0 / math.sqrt(SEQ * DP * T))
        total[1] = both_sum.astype(bf16)

        for j in range(1, 16):
            remote_to(total.at[1], done.at[mine], s_8, r_8, plane_peer(j)).start()
        pltpu.make_async_copy(total.at[1], done.at[mine], r_8).start()

    xhat = xhat_s[...]
    out = scale_s[:, 0:1] * (
        s - jnp.mean(s, -1, keepdims=True) - xhat * jnp.mean(s * xhat, -1, keepdims=True)
    )
    unorder = jnp.where(place_of(iota((1, T), 1)) == iota((T, T), 0), 1.0, 0.0).astype(bf16)
    out_s[0] = dot(unorder, out.astype(bf16)).astype(bf16)
    leave = pltpu.make_async_copy(out_s, out_ref, s_out)
    leave.start()
    drain(done, r_8)
    for p in range(2):
        for c in range(6):
            tile = done[p * 6 + c].astype(f32)
            merged_ref[2 * p, :, 128 * c : 128 * c + 128] = tile[:R]
            merged_ref[2 * p + 1, :, 128 * c : 128 * c + 128] = tile[R:]

    leave.wait()
    drain(same.at[pl.ds(0, (CHIPS - 1) * FAR)], s_kv)
    drain(other, s_qd)
    drain(recv2.at[pl.ds(0, (CHIPS - 1) * FAR)], s_2)
    drain(recv3.at[pl.ds(0, (CHIPS - 1) * FAR)], s_3)
    drain(rsame.at[pl.ds(0, (CHIPS - 1) * FAR)], s_4)
    drain(rother, s_5)

    @pl.when(mine < SLICES)
    def _():
        drain(one.at[pl.ds(0, SLICES - 1)], s_6)
        drain(two.at[pl.ds(0, 15)], s_7)
        drain(one.at[pl.ds(0, 15)], s_8)

    @pl.when(mine >= SLICES)
    def _():
        drain(one.at[pl.ds(0, SLICES)], s_6)


def hand_on_kernel(out_in, merged_in, out_ref, merged_ref, sems):
    copies = [
        pltpu.make_async_copy(out_in, out_ref, sems.at[0]),
        pltpu.make_async_copy(merged_in, merged_ref, sems.at[1]),
    ]
    for copy in copies:
        copy.start()
    for copy in copies:
        copy.wait()


def shape(*dims, kind=bf16):
    return jax.ShapeDtypeStruct(dims, kind)


def whole():
    return pl.BlockSpec(memory_space=pltpu.VMEM)


def far():
    return pl.BlockSpec(memory_space=pl.ANY)


def per_device(
    tiles, cotangent, gain, query_matrix, key_matrix, value_matrix, w_out,
    query_down_factor, query_up_factor, value_down_factor, value_up_factor, valid_count,
):
    buf = pltpu.VMEM
    sem = pltpu.SemaphoreType.DMA
    out, merged = pl.pallas_call(
        layer_kernel,
        out_shape=[shape(1, T, D), shape(4, R, D, kind=f32)],
        in_specs=[pl.BlockSpec(memory_space=pltpu.SMEM), whole(), far(), whole()] + [far()] * 4
        + [whole()] * 4,
        out_specs=[far(), whole()],
        scratch_shapes=[
            buf((1, T, D), bf16), buf((D, D), bf16), buf((D, D), bf16), buf((D, D), bf16),
            buf((D, D), bf16), sem((5,)), buf((1, T, D), bf16), sem,
            buf((T, D), f32), buf((T, 128), f32), buf((T, D), bf16), buf((2 * R, T), f32),
            buf((T, D), bf16), buf((T, D), bf16), buf((T, D), bf16),
            buf((D, T), bf16), buf((D, T), bf16), buf((D, T), bf16),
            buf((H, FAR, 256), bf16),
            buf((H, T, T), bf16), buf((H, T, T), bf16),
            buf((H // 2, PAIR, 256), bf16), buf((H // 2, PAIR, 256), bf16),
            buf((T, T), bf16), buf((PAIR, 256), bf16),
            buf((H, T), f32), buf((H, T), f32), buf((H, T), f32),
            buf((T, D), bf16), buf((D, T), f32), buf((D, PAIR), f32),
            buf((T, D), f32), buf((T, D), f32),
            buf((PAIR, D), bf16), buf((PAIR, D), bf16), buf((D, PAIR), bf16),
            buf((PAIR, D), f32), buf((PAIR, D), f32),
            buf((2, PAIR, D), bf16), buf((2, PAIR, D), bf16),
            buf((256, 256), bf16), buf((256, 128), bf16),
            buf((T, 128), bf16), buf((256, 128), bf16), buf((256, T), bf16),
            buf((256, 128), bf16), buf((256, 128), bf16),
            buf((FAR, 128), bf16), buf((256, 128), bf16),
            buf((256, 256), bf16), buf((256, 128), bf16),
            buf((256, 256), bf16), buf((256, 128), bf16),
            buf((SLICES, 16, 128), bf16), buf((16, 16, 128), bf16), buf((2, 16, 128), bf16),
            buf((16, 16, 128), bf16), buf((SLICES, 16, 128), bf16),
            sem, sem, sem, sem, sem((3,)), sem((3,)), sem, sem, sem, sem, sem, sem, sem, sem,
            sem, sem, sem, sem, sem, sem, sem, sem,
        ],
        compiler_params=pltpu.CompilerParams(
            vmem_limit_bytes=VMEM_LIMIT, collective_id=0, has_side_effects=True
        ),
        name="layer",
    )(
        valid_count, tiles, cotangent, gain, query_matrix, key_matrix, value_matrix, w_out,
        query_down_factor.T, query_up_factor, value_down_factor.T, value_up_factor,
    )
    return pl.pallas_call(
        hand_on_kernel,
        out_shape=[shape(1, T, D), shape(4, R, D, kind=f32)],
        in_specs=[whole()] * 2,
        out_specs=[far()] * 2,
        scratch_shapes=[sem((2,))],
        name="hand_on",
    )(out, merged)


def solution(mesh):
    placed = (P("dp", "seq", None),) * 2 + (P(),) * 9 + (P("dp"),)
    return jax.shard_map(
        per_device,
        mesh=mesh,
        in_specs=placed,
        out_specs=(P("dp", "seq", None), P()),
        check_vma=False,
    )
```

```python
import math

import jax
import jax.numpy as jnp
from jax import lax
from jax.experimental import pallas as pl
from jax.experimental.pallas import tpu as pltpu
from jax.sharding import PartitionSpec as P

T = 512
D = 768
H = 16
W = 48
R = 8
PAIR = 128
FAR = 16
SEQ = 32
DP = 8
CHIPS = 16
GROUPS = 2
SLICES = 12
PER = 8
EPS = 1e-5
LOG2E = math.log2(math.e)
SHARP = 1.0 / math.sqrt(W)
LN2 = math.log(2.0)
MESH = pl.DeviceIdType.MESH
f32 = jnp.float32
bf16 = jnp.bfloat16
VMEM_LIMIT = 56 * 1024 * 1024


def iota(shape, axis):
    return lax.broadcasted_iota(jnp.int32, shape, axis)


def dot(a, b):
    return jnp.dot(a, b, preferred_element_type=f32)


def dot_nt(a, b):
    return lax.dot_general(a, b, (((1,), (1,)), ((), ())), preferred_element_type=f32)


def place_of(row):
    return (row & 15) * 32 + ((row >> 4) & 7) * 4 + (row >> 7)


def order_matrix():
    place = place_of(iota((T, 128), 0))
    lane = iota((T, 128), 1)
    parts = [jnp.where(place == lane + 128 * c, 1.0, 0.0) for c in range(4)]
    return jnp.concatenate(parts, 1).astype(bf16)


def halves(value):
    upper = value.astype(bf16)
    lower = (value - upper.astype(f32)).astype(bf16)
    return upper, lower


def normalize(x):
    center = x - jnp.mean(x, -1, keepdims=True)
    inverse = lax.rsqrt(jnp.mean(center * center, -1, keepdims=True) + EPS)
    return center * inverse, inverse


def window(hh):
    low = W * hh
    first = low // 128
    last = (low + W - 1) // 128
    return first * 128, (last - first + 1) * 128, low - first * 128


def pair_window(p):
    low = 2 * W * p
    first = low // 128
    last = (low + 2 * W - 1) // 128
    return first * 128, (last - first + 1) * 128, low - first * 128


def lane_mask(width, off):
    lane = iota((1, width), 1)
    return jnp.where((lane >= off) & (lane < off + W), 1.0, 0.0).astype(bf16)


def pad_rows(block, off, width):
    parts = []
    if off:
        parts.append(jnp.zeros((off, block.shape[1]), block.dtype))
    parts.append(block)
    rest = width - off - block.shape[0]
    if rest:
        parts.append(jnp.zeros((rest, block.shape[1]), block.dtype))
    return jnp.concatenate(parts, 0)


def down_rows(qd_ref, vd_ref):
    return jnp.concatenate(
        [qd_ref[...].astype(f32), vd_ref[...].astype(f32), jnp.zeros((112, D), f32)], 0
    ).astype(bf16)


def up_padded(u_ref, at):
    return pad_rows(u_ref[...].astype(f32), at, 128).astype(bf16)


def layer_kernel(
    valid_ref, tiles_ref, cot_hbm, gain_ref, wq_hbm, wk_hbm, wv_hbm, wo_hbm,
    qd_ref, qu_ref, vd_ref, vu_ref,
    out_ref, merged_ref,
    cot_ref, wq_ref, wk_ref, wv_ref, wo_ref, s_in, out_s, s_out,
    xhat_s, scale_s, normed_s, lift_s, q_ref, k_ref, v_ref, qt_ref, kt_ref, dat_ref,
    sfar,
    e0, p0, e1, p1, mask0, mask1, tot, rsum, dlt, dap, dqt, dq1t, dk, dv,
    k1, v1, k1t, dk1, dv1, gsend, gback,
    same, other, kv, qda, fe, send2, recv2, send3, recv3, bsame, bother, rsame, rother,
    part, one, total, two, done,
    s_kv, r_kv, s_qd, r_qd, s_pair, r_pair, s_2, r_2, s_3, r_3, s_4, r_4, s_5, r_5, s_g, r_g,
    s_6, r_6, s_7, r_7, s_8, r_8,
):
    dp = lax.axis_index("dp")
    me = lax.axis_index("seq")
    chip = lax.div(me, 2)
    core = lax.rem(me, 2)
    mate = chip * 2 + (1 - core)
    column = lax.rem(me, 16)
    half = lax.div(me, 16)
    mine = dp * 2 + half
    valid = valid_ref[0]

    def plane_peer(j):
        there = lax.rem(mine + j, 16)
        return {"dp": lax.div(there, 2), "seq": lax.rem(there, 2) * 16 + column}

    def column_peer(j):
        return {"seq": half * 16 + lax.rem(column + j, 16)}

    barrier = pltpu.get_barrier_semaphore()

    for j in range(1, SEQ):
        pl.semaphore_signal(
            barrier, inc=1, device_id={"seq": lax.rem(me + j, SEQ)}, device_id_type=MESH
        )
    for j in range(1, 16):
        pl.semaphore_signal(barrier, inc=1, device_id=plane_peer(j), device_id_type=MESH)

    def remote_to(src, dst, send, recv, peer):
        return pltpu.make_async_remote_copy(
            src_ref=src, dst_ref=dst, send_sem=send, recv_sem=recv,
            device_id=peer, device_id_type=MESH,
        )

    def remote(src, dst, send, recv, peer):
        return remote_to(src, dst, send, recv, {"seq": peer})

    def drain(ref, sem):
        pltpu.make_async_copy(ref, ref, sem).wait()

    loads = [
        pltpu.make_async_copy(src, dst, s_in.at[i])
        for i, (src, dst) in enumerate(
            [(cot_hbm, cot_ref), (wo_hbm, wo_ref), (wq_hbm, wq_ref), (wk_hbm, wk_ref), (wv_hbm, wv_ref)]
        )
    ]
    for load in loads:
        load.start()

    order = order_matrix()
    x = dot(order, tiles_ref[0])
    loads[0].wait()
    loads[1].wait()
    cot = dot(order, cot_ref[0]).astype(bf16)
    da = dot_nt(cot, wo_ref[...]).astype(bf16)
    dat_ref[...] = da.T
    xhat, inverse_dev = normalize(x)
    xhat_s[...] = xhat
    scale_s[...] = jnp.broadcast_to(inverse_dev, (T, 128))
    normed = (xhat * gain_ref[...].astype(f32)).astype(bf16)
    normed_s[...] = normed
    down = down_rows(qd_ref, vd_ref)
    uq = up_padded(qu_ref, 0)
    uv = up_padded(vu_ref, R)
    lift = dot_nt(normed, down)
    both = jnp.concatenate(halves(lift), 1)
    lift_s[...] = lift.T[: 2 * R]
    loads[2].wait()
    loads[3].wait()
    loads[4].wait()
    q = dot(normed, wq_ref[...]) + 2.0 * dot(both, jnp.concatenate([uq, uq], 0))
    q = (q * (SHARP * LOG2E)).astype(bf16)
    q_ref[...] = q
    qt_ref[...] = q.T
    k = dot(normed, wk_ref[...]).astype(bf16)
    k_ref[...] = k
    kt_ref[...] = k.T
    v = (dot(normed, wv_ref[...]) + 2.0 * dot(both, jnp.concatenate([uv, uv], 0))).astype(bf16)
    v_ref[...] = v
    gap = jnp.zeros((FAR, 64 - W), f32)
    qf, kf, vf, df = (rows[:FAR].astype(f32) for rows in (q, k, v, da))
    for h in range(H):
        cut = slice(W * h, W * h + W)
        four = [kf[:, cut], gap, vf[:, cut], gap, qf[:, cut], gap, df[:, cut], gap]
        sfar[h] = jnp.concatenate(four, 1).astype(bf16)

    pl.semaphore_wait(barrier, SEQ - 1 + 15)

    def slot(c):
        return pl.ds(pl.multiple_of(c * FAR, FAR), FAR)

    def around(j):
        return lax.rem(chip + j, CHIPS)

    for j in range(CHIPS):
        there = around(j)
        if j:
            remote(sfar.at[there], same.at[slot(chip)], s_kv, r_kv, there * 2 + core).start()
        keys_only = sfar.at[there, :, pl.ds(0, 128)]
        remote(keys_only, other.at[slot(chip)], s_qd, r_qd, there * 2 + (1 - core)).start()
    pltpu.make_async_copy(sfar.at[chip], same.at[slot(chip)], r_kv).start()

    near = pl.ds(0, PAIR)
    pair_copies = [
        remote(k_ref.at[near], k1, s_pair.at[0], r_pair.at[0], mate),
        remote(v_ref.at[near], v1, s_pair.at[1], r_pair.at[1], mate),
        remote(kt_ref.at[:, near], k1t, s_pair.at[2], r_pair.at[2], mate),
    ]
    for copy in pair_copies:
        copy.start()

    row = iota((T, 128), 0)
    col = iota((T, 128), 1)
    seen = me * T + place_of(row) < valid
    for c in range(4):
        open0 = seen | (row == col + 128 * c)
        mask0[:, 128 * c : 128 * c + 128] = jnp.where(open0, jnp.inf, 0.0).astype(bf16)
    row = iota((PAIR, 2 * PAIR), 0)
    mask1[...] = jnp.where(mate * T + place_of(row) < valid, jnp.inf, 0.0).astype(bf16)

    def place(g, hh):
        base, width, off = window(hh)
        return pl.ds(g * 384 + base, width), pl.ds(g * 384 + W * hh, W), width, off

    def eight(g):
        return pl.ds(pl.multiple_of(g * PER, PER), PER)

    def column_sums(expo, dprob):
        expo = expo.astype(f32)
        return jnp.sum(expo, 0, keepdims=True), jnp.sum(expo * dprob, 0, keepdims=True)

    def forward0(heads):
        def operands(h, c):
            lanes, rows, width, off = place(h // PER, h % PER)
            cols = pl.ds(256 * c, 256)
            return (
                lanes, pad_rows(qt_ref[rows, cols], off, width),
                pad_rows(dat_ref[rows, cols], off, width),
            )

        def products(given, b):
            lanes, ask, grad = given
            block = pl.ds(128 * b, 128)
            return dot(k_ref[block, lanes], ask), dot(v_ref[block, lanes], grad)

        def fold(value):
            return jnp.sum(value.reshape(16, 8, 256), 0)

        steps = [(h, c, b) for h in heads for c in range(2) for b in range(4)]
        given = operands(heads[0], 0)
        score, dprob = products(given, 0)
        total = mixed = None
        for n, (h, c, b) in enumerate(steps):
            ahead = (None, None)
            if n + 1 < len(steps):
                after = steps[n + 1]
                if after[2] == 0:
                    given = operands(after[0], after[1])
                ahead = products(given, after[2])
            block = pl.ds(128 * b, 128)
            cols = pl.ds(256 * c, 256)
            expo = jnp.minimum(jnp.exp2(score).astype(bf16), mask0[block, cols])
            if c == 0 and b == 0:
                corner = expo[:, :PAIR]
                expo = jnp.concatenate([corner + corner, expo[:, PAIR:]], 1)
            e0[h, block, cols] = expo
            p0[h, block, cols] = dprob.astype(bf16)
            wide = expo.astype(f32)
            if b == 0:
                total, mixed = fold(wide), fold(wide * dprob)
            else:
                total, mixed = total + fold(wide), mixed + fold(wide * dprob)
            if b == 3:
                tot[h : h + 1, cols] = jnp.sum(total, 0, keepdims=True)
                rsum[h : h + 1, cols] = jnp.sum(mixed, 0, keepdims=True)
            score, dprob = ahead

    def pair_place(g, p):
        base, width, off = pair_window(p)
        lanes = pl.ds(g * 384 + base, width)
        low = pl.ds(pl.multiple_of(g * 384 + 2 * W * p, 16), W)
        high = pl.ds(pl.multiple_of(g * 384 + 2 * W * p + W, 16), W)
        both = pl.ds(pl.multiple_of(g * 384 + 2 * W * p, 16), 2 * W)
        return lanes, low, high, both, width, off

    def side_by_side(low, high, off, width):
        none = jnp.zeros((W, PAIR), bf16)
        block = jnp.concatenate(
            [jnp.concatenate([low, none], 1), jnp.concatenate([none, high], 1)], 0
        )
        return pad_rows(block, off, width)

    def stacked(rows, off, width):
        return jnp.concatenate([rows * lane_mask(width, off), rows * lane_mask(width, off + W)], 0)

    def forward1(g):
        totals, sums = [], []
        for p in range(PER // 2):
            lanes, low, high, both, width, off = pair_place(g, p)
            ask = side_by_side(qt_ref[low, near], qt_ref[high, near], off, width)
            given = side_by_side(dat_ref[low, near], dat_ref[high, near], off, width)
            expo = jnp.minimum(jnp.exp2(dot(k1[:, lanes], ask)).astype(bf16), mask1[...])
            dprob = dot(v1[:, lanes], given)
            e1[g * (PER // 2) + p] = expo
            p1[g * (PER // 2) + p] = dprob.astype(bf16)
            here, mixed = column_sums(expo, dprob)
            totals += [here[:, :PAIR], here[:, PAIR:]]
            sums += [mixed[:, :PAIR], mixed[:, PAIR:]]
        tot[eight(g), near] += jnp.concatenate(totals, 0)
        rsum[eight(g), near] += jnp.concatenate(sums, 0)

    forward0(range(0, 10))

    drain(same, r_kv)
    drain(other, r_qd)
    kv[pl.ds(0, 256)] = same[:, :128]
    kv[pl.ds(256, 256)] = other[...]
    qda[...] = same[:, 128:]
    lane = iota((1, 128), 1)
    low = jnp.where(lane < 64, 1.0, 0.0).astype(bf16)
    high = jnp.where(lane >= 64, 1.0, 0.0).astype(bf16)
    i2 = iota((256, T), 0)
    j2 = iota((1, T), 1)
    j2_core = (j2 >> 8) * (1 - core) + (1 - (j2 >> 8)) * core
    j2_pos = (((j2 & 255) >> 4) * 2 + j2_core) * T + (j2 & 15) * 32
    open2 = (j2_pos < valid) | (j2 == i2)
    far_expo = jnp.exp2(dot_nt(qda[...], kv[...] * low))
    far_expo = jnp.where(open2, far_expo, 0.0).astype(bf16)
    fe[...] = far_expo
    first_lane = jnp.where(lane == 0, 1.0, 0.0).astype(bf16)
    far_mixed = dot(far_expo, kv[...] * high + first_lane)
    far_r = jnp.sum(
        jnp.where(lane >= 64, qda[...].astype(f32) * far_mixed, 0.0), 1, keepdims=True
    )
    far_t = far_mixed[:, 0:1]
    far_parts = halves(far_t) + halves(far_r)
    packed = jnp.zeros((256, 128), f32)
    for i in range(4):
        packed = packed + jnp.where(lane == 16 * i + chip, far_parts[i].astype(f32), 0.0)
    send2[...] = packed.astype(bf16)

    for j in range(1, CHIPS):
        there = around(j)
        remote(send2.at[slot(there)], recv2.at[slot(chip)], s_2, r_2, there * 2 + core).start()
    pltpu.make_async_copy(send2.at[slot(chip)], recv2.at[slot(chip)], r_2).start()

    forward0(range(10, 16))
    for copy in pair_copies:
        copy.wait()
    for g in range(GROUPS):
        forward1(g)

    drain(recv2, r_2)
    gathered = recv2[pl.ds(0, FAR)].astype(f32)
    for c in range(1, CHIPS):
        gathered = gathered + recv2[pl.ds(c * FAR, FAR)].astype(f32)
    turned = jnp.concatenate([gathered, jnp.zeros((PAIR - FAR, 128), f32)], 0).T
    tot[:, near] += turned[:16] + turned[16:32]
    inverse = 1.0 / tot[...]
    tot[...] = inverse
    rsum[:, near] += turned[32:48] + turned[48:64]
    dlt[...] = rsum[...] * inverse * inverse
    scale_parts = [part.astype(f32) for part in halves(tot[:, near]) + halves(dlt[:, near])]
    scale_parts.append(jnp.zeros((64, 128), f32))
    send3[...] = jnp.concatenate(scale_parts, 0).T[:FAR].astype(bf16)

    for j in range(1, CHIPS):
        there = around(j)
        remote(send3, recv3.at[slot(chip)], s_3, r_3, there * 2 + core).start()
    pltpu.make_async_copy(send3, recv3.at[slot(chip)], r_3).start()
    scaled = []
    for h in range(H):
        rows = pl.ds(W * h, W)
        scaled.append((dat_ref[rows, :].astype(f32) * tot[h : h + 1, :]).astype(bf16))
    dap[...] = jnp.concatenate(scaled, 0).T

    def gather_in(ref, lanes, width, value, fresh):
        if width == 128:
            if fresh:
                ref[:, lanes] = value
            else:
                ref[:, lanes] += value
        else:
            ref[:, pl.ds(lanes.start, 128)] += value[:, :128]
            ref[:, pl.ds(lanes.start + 128, 128)] = value[:, 128:]

    def dscores(h):
        dprob = p0[h].astype(f32) * tot[h : h + 1, :] - dlt[h : h + 1, :]
        return e0[h] * dprob.astype(bf16)

    def backward0(heads):
        dscore = dscores(heads[0])
        for h in heads:
            lanes, rows, width, off = place(h // PER, h % PER)
            value = dot(e0[h], dap[:, lanes] * lane_mask(width, off))
            gather_in(dv, lanes, width, value, h % PER == 0)
            ahead = dscores(h + 1) if h + 1 in heads else None
            p0[h] = dscore
            dqt[rows, :] = dot(kt_ref[rows, :], dscore)
            dscore = ahead

    def backward1(g):
        for p in range(PER // 2):
            lanes, low, high, both, width, off = pair_place(g, p)
            expo = e1[g * (PER // 2) + p]
            a, b = g * PER + 2 * p, g * PER + 2 * p + 1
            scale = jnp.concatenate([tot[a : a + 1, near], tot[b : b + 1, near]], 1)
            delta = jnp.concatenate([dlt[a : a + 1, near], dlt[b : b + 1, near]], 1)
            dprob = p1[g * (PER // 2) + p].astype(f32) * scale - delta
            dscore = expo * dprob.astype(bf16)
            dq = dot(k1t[both, :], dscore)
            dq1t[low, :] = dq[:W, :PAIR]
            dq1t[high, :] = dq[W:, PAIR:]
            value = dot(expo, stacked(dap[near, lanes], off, width))
            gather_in(dv1, lanes, width, value, p == 0)
            value = dot(dscore, stacked(q_ref[near, lanes], off, width))
            gather_in(dk1, lanes, width, value, p == 0)

    def keys0(g):
        for hh in range(PER):
            lanes, rows, width, off = place(g, hh)
            value = dot(p0[g * PER + hh], q_ref[:, lanes] * lane_mask(width, off))
            gather_in(dk, lanes, width, value, hh == 0)

    for g in range(GROUPS):
        backward1(g)
    gsend[0] = dk1[...].astype(bf16)
    gsend[1] = dv1[...].astype(bf16)
    grad_copy = remote(gsend, gback, s_g, r_g, mate)
    grad_copy.start()
    backward0(range(0, 4))

    drain(recv3, r_3)
    scales = recv3[...].astype(f32)
    for_head = (lane & 15) == chip
    far_inv = jnp.sum(jnp.where(for_head & (lane < 32), scales, 0.0), 1, keepdims=True)
    far_del = jnp.sum(jnp.where(for_head & (lane >= 32), scales, 0.0), 1, keepdims=True)
    far_grads = jnp.where(lane >= 64, qda[...].astype(f32) * far_inv, 0.0).astype(bf16)
    far_back = fe[...].astype(f32)
    far_ds = far_back * (dot_nt(far_grads, kv[...] * high) - far_del)
    back_kv = (
        dot(far_ds.T.astype(bf16), qda[...] * low) + dot(far_back.T.astype(bf16), far_grads)
    ).astype(bf16)
    bsame[:, :128] = back_kv[:256]
    bsame[:, 128:] = dot(far_ds.astype(bf16), kv[...] * low).astype(bf16)
    bother[...] = back_kv[256:]
    for j in range(CHIPS):
        there = around(j)
        if j:
            remote(
                bsame.at[slot(there)], rsame.at[slot(chip)], s_4, r_4, there * 2 + core
            ).start()
        remote(
            bother.at[slot(there)], rother.at[slot(chip)], s_5, r_5, there * 2 + (1 - core)
        ).start()
    pltpu.make_async_copy(bsame.at[slot(chip)], rsame.at[slot(chip)], r_4).start()

    backward0(range(4, 16))

    grad_copy.wait()
    drain(rsame, r_4)
    drain(rother, r_5)
    keys_back, values_back, asks_back = [], [], []
    for h in range(H):
        both_back = rsame[pl.ds(h * FAR, FAR)].astype(f32)
        here = both_back[:, :128] + rother[pl.ds(h * FAR, FAR)].astype(f32)
        keys_back.append(here[:, :W])
        values_back.append(here[:, 64 : 64 + W])
        asks_back.append(both_back[:, 128 : 128 + W])
    few = pl.ds(0, FAR)
    dv[near] += gback[1].astype(f32)
    dv[few] += jnp.concatenate(values_back, 1)
    dqt[:, near] += dq1t[...]
    gq = (dqt[...] * SHARP).astype(bf16).T
    first_rows = dqt[:, near].T[:FAR] + jnp.concatenate(asks_back, 1)
    gq = jnp.concatenate([(first_rows * SHARP).astype(bf16), gq[FAR:]], 0)
    gv = dv[...].astype(bf16)
    back = dot_nt(gq, uq) + dot_nt(gv, uv)
    back_both = jnp.concatenate(halves(back), 1)
    bu, bl = halves(back.T[: 2 * R])
    lu, ll = halves(lift_s[...])
    from_back = dot(jnp.concatenate([bu, bl], 0), normed_s[...])
    from_back = 2.0 * (from_back[:16] + from_back[16:])
    lifts = jnp.concatenate([lu, ll], 0)
    from_q = dot(lifts, gq)
    from_q = 2.0 * (from_q[:R] + from_q[16 : 16 + R])
    from_v = dot(lifts, gv)
    from_v = 2.0 * (from_v[R:16] + from_v[16 + R : 32])
    pairs = [
        jnp.concatenate([from_back[:R], from_q], 0), jnp.concatenate([from_back[R:16], from_v], 0)
    ]
    for p in range(2):
        for c in range(6):
            part[p * 6 + c] = pairs[p][:, 128 * c : 128 * c + 128].astype(bf16)

    def first(j, carry):
        there = lax.rem(mine + j, 16)

        @pl.when(there < SLICES)
        def _():
            remote_to(part.at[there], one.at[mine], s_6, r_6, plane_peer(j)).start()

        return carry

    lax.fori_loop(1, 16, first, 0)

    @pl.when(mine < SLICES)
    def _():
        pltpu.make_async_copy(part.at[mine], one.at[mine], r_6).start()

    for g in range(GROUPS):
        keys0(g)

    @pl.when(mine < SLICES)
    def _():
        drain(one, r_6)
        total[0] = jnp.sum(one[...].astype(f32), 0).astype(bf16)

        for j in range(1, 16):
            remote_to(total.at[0], two.at[column], s_7, r_7, column_peer(j)).start()
        pltpu.make_async_copy(total.at[0], two.at[column], r_7).start()

    dk[near] += gback[0].astype(f32)
    dk[few] += jnp.concatenate(keys_back, 1)
    gk = (dk[...] * LN2).astype(bf16)
    grad = (
        dot_nt(gq, wq_ref[...])
        + dot_nt(gk, wk_ref[...])
        + dot_nt(gv, wv_ref[...])
        + 2.0 * dot(back_both, jnp.concatenate([down, down], 0))
    )
    s = grad * gain_ref[...].astype(f32)

    @pl.when(mine < SLICES)
    def _():
        drain(two, r_7)
        both_sum = jnp.sum(two[...].astype(f32), 0) * (1.0 / math.sqrt(SEQ * DP * T))
        total[1] = both_sum.astype(bf16)

        for j in range(1, 16):
            remote_to(total.at[1], done.at[mine], s_8, r_8, plane_peer(j)).start()
        pltpu.make_async_copy(total.at[1], done.at[mine], r_8).start()

    xhat = xhat_s[...]
    out = scale_s[:, 0:1] * (
        s - jnp.mean(s, -1, keepdims=True) - xhat * jnp.mean(s * xhat, -1, keepdims=True)
    )
    unorder = jnp.where(place_of(iota((1, T), 1)) == iota((T, T), 0), 1.0, 0.0).astype(bf16)
    out_s[0] = dot(unorder, out.astype(bf16)).astype(bf16)
    leave = pltpu.make_async_copy(out_s, out_ref, s_out)
    leave.start()
    drain(done, r_8)
    for p in range(2):
        for c in range(6):
            tile = done[p * 6 + c].astype(f32)
            merged_ref[2 * p, :, 128 * c : 128 * c + 128] = tile[:R]
            merged_ref[2 * p + 1, :, 128 * c : 128 * c + 128] = tile[R:]

    leave.wait()
    drain(same.at[pl.ds(0, (CHIPS - 1) * FAR)], s_kv)
    drain(other, s_qd)
    drain(recv2.at[pl.ds(0, (CHIPS - 1) * FAR)], s_2)
    drain(recv3.at[pl.ds(0, (CHIPS - 1) * FAR)], s_3)
    drain(rsame.at[pl.ds(0, (CHIPS - 1) * FAR)], s_4)
    drain(rother, s_5)

    @pl.when(mine < SLICES)
    def _():
        drain(one.at[pl.ds(0, SLICES - 1)], s_6)
        drain(two.at[pl.ds(0, 15)], s_7)
        drain(one.at[pl.ds(0, 15)], s_8)

    @pl.when(mine >= SLICES)
    def _():
        drain(one.at[pl.ds(0, SLICES)], s_6)


def hand_on_kernel(out_in, merged_in, out_ref, merged_ref, sems):
    copies = [
        pltpu.make_async_copy(out_in, out_ref, sems.at[0]),
        pltpu.make_async_copy(merged_in, merged_ref, sems.at[1]),
    ]
    for copy in copies:
        copy.start()
    for copy in copies:
        copy.wait()


def shape(*dims, kind=bf16):
    return jax.ShapeDtypeStruct(dims, kind)


def whole():
    return pl.BlockSpec(memory_space=pltpu.VMEM)


def far():
    return pl.BlockSpec(memory_space=pl.ANY)


def per_device(
    tiles, cotangent, gain, query_matrix, key_matrix, value_matrix, w_out,
    query_down_factor, query_up_factor, value_down_factor, value_up_factor, valid_count,
):
    buf = pltpu.VMEM
    sem = pltpu.SemaphoreType.DMA
    out, merged = pl.pallas_call(
        layer_kernel,
        out_shape=[shape(1, T, D), shape(4, R, D, kind=f32)],
        in_specs=[pl.BlockSpec(memory_space=pltpu.SMEM), whole(), far(), whole()] + [far()] * 4
        + [whole()] * 4,
        out_specs=[far(), whole()],
        scratch_shapes=[
            buf((1, T, D), bf16), buf((D, D), bf16), buf((D, D), bf16), buf((D, D), bf16),
            buf((D, D), bf16), sem((5,)), buf((1, T, D), bf16), sem,
            buf((T, D), f32), buf((T, 128), f32), buf((T, D), bf16), buf((2 * R, T), f32),
            buf((T, D), bf16), buf((T, D), bf16), buf((T, D), bf16),
            buf((D, T), bf16), buf((D, T), bf16), buf((D, T), bf16),
            buf((H, FAR, 256), bf16),
            buf((H, T, T), bf16), buf((H, T, T), bf16),
            buf((H // 2, PAIR, 256), bf16), buf((H // 2, PAIR, 256), bf16),
            buf((T, T), bf16), buf((PAIR, 256), bf16),
            buf((H, T), f32), buf((H, T), f32), buf((H, T), f32),
            buf((T, D), bf16), buf((D, T), f32), buf((D, PAIR), f32),
            buf((T, D), f32), buf((T, D), f32),
            buf((PAIR, D), bf16), buf((PAIR, D), bf16), buf((D, PAIR), bf16),
            buf((PAIR, D), f32), buf((PAIR, D), f32),
            buf((2, PAIR, D), bf16), buf((2, PAIR, D), bf16),
            buf((256, 256), bf16), buf((256, 128), bf16),
            buf((T, 128), bf16), buf((256, 128), bf16), buf((256, T), bf16),
            buf((256, 128), bf16), buf((256, 128), bf16),
            buf((FAR, 128), bf16), buf((256, 128), bf16),
            buf((256, 256), bf16), buf((256, 128), bf16),
            buf((256, 256), bf16), buf((256, 128), bf16),
            buf((SLICES, 16, 128), bf16), buf((16, 16, 128), bf16), buf((2, 16, 128), bf16),
            buf((16, 16, 128), bf16), buf((SLICES, 16, 128), bf16),
            sem, sem, sem, sem, sem((3,)), sem((3,)), sem, sem, sem, sem, sem, sem, sem, sem,
            sem, sem, sem, sem, sem, sem, sem, sem,
        ],
        compiler_params=pltpu.CompilerParams(
            vmem_limit_bytes=VMEM_LIMIT, collective_id=0, has_side_effects=True
        ),
        name="layer",
    )(
        valid_count, tiles, cotangent, gain, query_matrix, key_matrix, value_matrix, w_out,
        query_down_factor.T, query_up_factor, value_down_factor.T, value_up_factor,
    )
    return pl.pallas_call(
        hand_on_kernel,
        out_shape=[shape(1, T, D), shape(4, R, D, kind=f32)],
        in_specs=[whole()] * 2,
        out_specs=[far()] * 2,
        scratch_shapes=[sem((2,))],
        name="hand_on",
    )(out, merged)


def solution(mesh):
    placed = (P("dp", "seq", None),) * 2 + (P(),) * 9 + (P("dp"),)
    return jax.shard_map(
        per_device,
        mesh=mesh,
        in_specs=placed,
        out_specs=(P("dp", "seq", None), P()),
        check_vma=False,
    )
```

```python
import math

import jax
import jax.numpy as jnp
from jax import lax
from jax.experimental import pallas as pl
from jax.experimental.pallas import tpu as pltpu
from jax.sharding import PartitionSpec as P

T = 512
D = 768
H = 16
W = 48
R = 8
PAIR = 128
FAR = 16
SEQ = 32
DP = 8
CHIPS = 16
GROUPS = 2
SLICES = 12
PER = 8
EPS = 1e-5
LOG2E = math.log2(math.e)
SHARP = 1.0 / math.sqrt(W)
LN2 = math.log(2.0)
MESH = pl.DeviceIdType.MESH
f32 = jnp.float32
bf16 = jnp.bfloat16
VMEM_LIMIT = 56 * 1024 * 1024


def iota(shape, axis):
    return lax.broadcasted_iota(jnp.int32, shape, axis)


def dot(a, b):
    return jnp.dot(a, b, preferred_element_type=f32)


def dot_nt(a, b):
    return lax.dot_general(a, b, (((1,), (1,)), ((), ())), preferred_element_type=f32)


def place_of(row):
    return (row & 15) * 32 + ((row >> 4) & 7) * 4 + (row >> 7)


def order_matrix(first, count):
    place = place_of(first + iota((count, 128), 0))
    lane = iota((count, 128), 1)
    parts = [jnp.where(place == lane + 128 * c, 1.0, 0.0) for c in range(4)]
    return jnp.concatenate(parts, 1).astype(bf16)


def halves(value):
    upper = value.astype(bf16)
    lower = (value - upper.astype(f32)).astype(bf16)
    return upper, lower


def normalize(x):
    center = x - jnp.mean(x, -1, keepdims=True)
    inverse = lax.rsqrt(jnp.mean(center * center, -1, keepdims=True) + EPS)
    return center * inverse, inverse


def window(hh):
    low = W * hh
    first = low // 128
    last = (low + W - 1) // 128
    return first * 128, (last - first + 1) * 128, low - first * 128


def pair_window(p):
    low = 2 * W * p
    first = low // 128
    last = (low + 2 * W - 1) // 128
    return first * 128, (last - first + 1) * 128, low - first * 128


def lane_mask(width, off):
    lane = iota((1, width), 1)
    return jnp.where((lane >= off) & (lane < off + W), 1.0, 0.0).astype(bf16)


def pad_rows(block, off, width):
    parts = []
    if off:
        parts.append(jnp.zeros((off, block.shape[1]), block.dtype))
    parts.append(block)
    rest = width - off - block.shape[0]
    if rest:
        parts.append(jnp.zeros((rest, block.shape[1]), block.dtype))
    return jnp.concatenate(parts, 0)


def down_rows(qd_ref, vd_ref):
    return jnp.concatenate(
        [qd_ref[...].astype(f32), vd_ref[...].astype(f32), jnp.zeros((112, D), f32)], 0
    ).astype(bf16)


def up_padded(u_ref, at):
    return pad_rows(u_ref[...].astype(f32), at, 128).astype(bf16)


def layer_kernel(
    valid_ref, tiles_ref, cot_hbm, gain_ref, wq_hbm, wk_hbm, wv_hbm, wo_hbm,
    qd_ref, qu_ref, vd_ref, vu_ref,
    out_ref, merged_ref,
    cot_ref, wq_ref, wk_ref, wv_ref, wo_ref, s_in, out_s, s_out,
    xhat_s, scale_s, normed_s, lift_s, q_ref, k_ref, v_ref, qt_ref, kt_ref, dat_ref,
    sfar,
    e0, p0, e1, p1, mask0, mask1, tot, rsum, dlt, dap, dqt, dq1t, dk, dv,
    k1, v1, k1t, dk1, dv1, gsend, gback,
    same, other, kv, qda, fe, send2, recv2, send3, recv3, bsame, bother, rsame, rother,
    part, one, total, two, done,
    s_kv, r_kv, s_qd, r_qd, s_pair, r_pair, s_2, r_2, s_3, r_3, s_4, r_4, s_5, r_5, s_g, r_g,
    s_6, r_6, s_7, r_7, s_8, r_8,
):
    dp = lax.axis_index("dp")
    me = lax.axis_index("seq")
    chip = lax.div(me, 2)
    core = lax.rem(me, 2)
    mate = chip * 2 + (1 - core)
    column = lax.rem(me, 16)
    half = lax.div(me, 16)
    mine = dp * 2 + half
    valid = valid_ref[0]

    def plane_peer(j):
        there = lax.rem(mine + j, 16)
        return {"dp": lax.div(there, 2), "seq": lax.rem(there, 2) * 16 + column}

    def column_peer(j):
        return {"seq": half * 16 + lax.rem(column + j, 16)}

    barrier = pltpu.get_barrier_semaphore()

    for j in range(1, SEQ):
        pl.semaphore_signal(
            barrier, inc=1, device_id={"seq": lax.rem(me + j, SEQ)}, device_id_type=MESH
        )
    for j in range(1, 16):
        pl.semaphore_signal(barrier, inc=1, device_id=plane_peer(j), device_id_type=MESH)

    def remote_to(src, dst, send, recv, peer):
        return pltpu.make_async_remote_copy(
            src_ref=src, dst_ref=dst, send_sem=send, recv_sem=recv,
            device_id=peer, device_id_type=MESH,
        )

    def remote(src, dst, send, recv, peer):
        return remote_to(src, dst, send, recv, {"seq": peer})

    def drain(ref, sem):
        pltpu.make_async_copy(ref, ref, sem).wait()

    loads = [
        pltpu.make_async_copy(src, dst, s_in.at[i])
        for i, (src, dst) in enumerate(
            [(cot_hbm, cot_ref), (wo_hbm, wo_ref), (wq_hbm, wq_ref), (wk_hbm, wk_ref), (wv_hbm, wv_ref)]
        )
    ]
    for load in loads:
        load.start()

    down = down_rows(qd_ref, vd_ref)
    uq = up_padded(qu_ref, 0)
    uv = up_padded(vu_ref, R)

    def project(first, count, arrive):
        some = pl.ds(first, count)
        order = order_matrix(first, count)
        x = dot(order, tiles_ref[0])
        arrive(0, 1)
        cot = dot(order, cot_ref[0]).astype(bf16)
        da = dot_nt(cot, wo_ref[...]).astype(bf16)
        dat_ref[:, some] = da.T
        xhat, inverse_dev = normalize(x)
        xhat_s[some] = xhat
        scale_s[some] = jnp.broadcast_to(inverse_dev, (count, 128))
        normed = (xhat * gain_ref[...].astype(f32)).astype(bf16)
        normed_s[some] = normed
        lift = dot_nt(normed, down)
        both = jnp.concatenate(halves(lift), 1)
        lift_s[:, some] = lift.T[: 2 * R]
        arrive(2, 3, 4)
        q = dot(normed, wq_ref[...]) + 2.0 * dot(both, jnp.concatenate([uq, uq], 0))
        q = (q * (SHARP * LOG2E)).astype(bf16)
        q_ref[some] = q
        qt_ref[:, some] = q.T
        k = dot(normed, wk_ref[...]).astype(bf16)
        k_ref[some] = k
        kt_ref[:, some] = k.T
        v = (dot(normed, wv_ref[...]) + 2.0 * dot(both, jnp.concatenate([uv, uv], 0))).astype(bf16)
        v_ref[some] = v
        return q, k, v, da

    def arrive(*which):
        for i in which:
            loads[i].wait()

    q, k, v, da = project(0, PAIR, arrive)
    gap = jnp.zeros((FAR, 64 - W), f32)
    qf, kf, vf, df = (rows[:FAR].astype(f32) for rows in (q, k, v, da))
    for h in range(H):
        cut = slice(W * h, W * h + W)
        four = [kf[:, cut], gap, vf[:, cut], gap, qf[:, cut], gap, df[:, cut], gap]
        sfar[h] = jnp.concatenate(four, 1).astype(bf16)

    pl.semaphore_wait(barrier, SEQ - 1 + 15)

    def slot(c):
        return pl.ds(pl.multiple_of(c * FAR, FAR), FAR)

    def around(j):
        return lax.rem(chip + j, CHIPS)

    for j in range(CHIPS):
        there = around(j)
        if j:
            remote(sfar.at[there], same.at[slot(chip)], s_kv, r_kv, there * 2 + core).start()
        keys_only = sfar.at[there, :, pl.ds(0, 128)]
        remote(keys_only, other.at[slot(chip)], s_qd, r_qd, there * 2 + (1 - core)).start()
    pltpu.make_async_copy(sfar.at[chip], same.at[slot(chip)], r_kv).start()

    near = pl.ds(0, PAIR)
    pair_copies = [
        remote(k_ref.at[near], k1, s_pair.at[0], r_pair.at[0], mate),
        remote(v_ref.at[near], v1, s_pair.at[1], r_pair.at[1], mate),
        remote(kt_ref.at[:, near], k1t, s_pair.at[2], r_pair.at[2], mate),
    ]
    for copy in pair_copies:
        copy.start()

    project(PAIR, T - PAIR, lambda *which: None)

    row = iota((T, 128), 0)
    col = iota((T, 128), 1)
    seen = me * T + place_of(row) < valid
    for c in range(4):
        open0 = seen | (row == col + 128 * c)
        mask0[:, 128 * c : 128 * c + 128] = jnp.where(open0, jnp.inf, 0.0).astype(bf16)
    row = iota((PAIR, 2 * PAIR), 0)
    mask1[...] = jnp.where(mate * T + place_of(row) < valid, jnp.inf, 0.0).astype(bf16)

    def place(g, hh):
        base, width, off = window(hh)
        return pl.ds(g * 384 + base, width), pl.ds(g * 384 + W * hh, W), width, off

    def eight(g):
        return pl.ds(pl.multiple_of(g * PER, PER), PER)

    def column_sums(expo, dprob):
        expo = expo.astype(f32)
        return jnp.sum(expo, 0, keepdims=True), jnp.sum(expo * dprob, 0, keepdims=True)

    def forward0(heads):
        def operands(h, c):
            lanes, rows, width, off = place(h // PER, h % PER)
            cols = pl.ds(256 * c, 256)
            return (
                lanes, pad_rows(qt_ref[rows, cols], off, width),
                pad_rows(dat_ref[rows, cols], off, width),
            )

        def products(given, b):
            lanes, ask, grad = given
            block = pl.ds(128 * b, 128)
            return dot(k_ref[block, lanes], ask), dot(v_ref[block, lanes], grad)

        def fold(value):
            return jnp.sum(value.reshape(16, 8, 256), 0)

        steps = [(h, c, b) for h in heads for c in range(2) for b in range(4)]
        given = operands(heads[0], 0)
        score, dprob = products(given, 0)
        total = mixed = None
        for n, (h, c, b) in enumerate(steps):
            ahead = (None, None)
            if n + 1 < len(steps):
                after = steps[n + 1]
                if after[2] == 0:
                    given = operands(after[0], after[1])
                ahead = products(given, after[2])
            block = pl.ds(128 * b, 128)
            cols = pl.ds(256 * c, 256)
            expo = jnp.minimum(jnp.exp2(score).astype(bf16), mask0[block, cols])
            if c == 0 and b == 0:
                corner = expo[:, :PAIR]
                expo = jnp.concatenate([corner + corner, expo[:, PAIR:]], 1)
            e0[h, block, cols] = expo
            p0[h, block, cols] = dprob.astype(bf16)
            wide = expo.astype(f32)
            if b == 0:
                total, mixed = fold(wide), fold(wide * dprob)
            else:
                total, mixed = total + fold(wide), mixed + fold(wide * dprob)
            if b == 3:
                tot[h : h + 1, cols] = jnp.sum(total, 0, keepdims=True)
                rsum[h : h + 1, cols] = jnp.sum(mixed, 0, keepdims=True)
            score, dprob = ahead

    def pair_place(g, p):
        base, width, off = pair_window(p)
        lanes = pl.ds(g * 384 + base, width)
        low = pl.ds(pl.multiple_of(g * 384 + 2 * W * p, 16), W)
        high = pl.ds(pl.multiple_of(g * 384 + 2 * W * p + W, 16), W)
        both = pl.ds(pl.multiple_of(g * 384 + 2 * W * p, 16), 2 * W)
        return lanes, low, high, both, width, off

    def side_by_side(low, high, off, width):
        none = jnp.zeros((W, PAIR), bf16)
        block = jnp.concatenate(
            [jnp.concatenate([low, none], 1), jnp.concatenate([none, high], 1)], 0
        )
        return pad_rows(block, off, width)

    def stacked(rows, off, width):
        return jnp.concatenate([rows * lane_mask(width, off), rows * lane_mask(width, off + W)], 0)

    def forward1(g):
        totals, sums = [], []
        for p in range(PER // 2):
            lanes, low, high, both, width, off = pair_place(g, p)
            ask = side_by_side(qt_ref[low, near], qt_ref[high, near], off, width)
            given = side_by_side(dat_ref[low, near], dat_ref[high, near], off, width)
            expo = jnp.minimum(jnp.exp2(dot(k1[:, lanes], ask)).astype(bf16), mask1[...])
            dprob = dot(v1[:, lanes], given)
            e1[g * (PER // 2) + p] = expo
            p1[g * (PER // 2) + p] = dprob.astype(bf16)
            here, mixed = column_sums(expo, dprob)
            totals += [here[:, :PAIR], here[:, PAIR:]]
            sums += [mixed[:, :PAIR], mixed[:, PAIR:]]
        tot[eight(g), near] += jnp.concatenate(totals, 0)
        rsum[eight(g), near] += jnp.concatenate(sums, 0)

    forward0(range(0, 6))

    drain(same, r_kv)
    drain(other, r_qd)
    kv[pl.ds(0, 256)] = same[:, :128]
    kv[pl.ds(256, 256)] = other[...]
    qda[...] = same[:, 128:]
    lane = iota((1, 128), 1)
    low = jnp.where(lane < 64, 1.0, 0.0).astype(bf16)
    high = jnp.where(lane >= 64, 1.0, 0.0).astype(bf16)
    i2 = iota((256, T), 0)
    j2 = iota((1, T), 1)
    j2_core = (j2 >> 8) * (1 - core) + (1 - (j2 >> 8)) * core
    j2_pos = (((j2 & 255) >> 4) * 2 + j2_core) * T + (j2 & 15) * 32
    open2 = (j2_pos < valid) | (j2 == i2)
    far_expo = jnp.exp2(dot_nt(qda[...], kv[...] * low))
    far_expo = jnp.where(open2, far_expo, 0.0).astype(bf16)
    fe[...] = far_expo
    first_lane = jnp.where(lane == 0, 1.0, 0.0).astype(bf16)
    far_mixed = dot(far_expo, kv[...] * high + first_lane)
    far_r = jnp.sum(
        jnp.where(lane >= 64, qda[...].astype(f32) * far_mixed, 0.0), 1, keepdims=True
    )
    far_t = far_mixed[:, 0:1]
    far_parts = halves(far_t) + halves(far_r)
    packed = jnp.zeros((256, 128), f32)
    for i in range(4):
        packed = packed + jnp.where(lane == 16 * i + chip, far_parts[i].astype(f32), 0.0)
    send2[...] = packed.astype(bf16)

    for j in range(1, CHIPS):
        there = around(j)
        remote(send2.at[slot(there)], recv2.at[slot(chip)], s_2, r_2, there * 2 + core).start()
    pltpu.make_async_copy(send2.at[slot(chip)], recv2.at[slot(chip)], r_2).start()

    forward0(range(6, 16))
    for copy in pair_copies:
        copy.wait()
    for g in range(GROUPS):
        forward1(g)

    drain(recv2, r_2)
    gathered = recv2[pl.ds(0, FAR)].astype(f32)
    for c in range(1, CHIPS):
        gathered = gathered + recv2[pl.ds(c * FAR, FAR)].astype(f32)
    turned = jnp.concatenate([gathered, jnp.zeros((PAIR - FAR, 128), f32)], 0).T
    tot[:, near] += turned[:16] + turned[16:32]
    inverse = 1.0 / tot[...]
    tot[...] = inverse
    rsum[:, near] += turned[32:48] + turned[48:64]
    dlt[...] = rsum[...] * inverse * inverse
    scale_parts = [part.astype(f32) for part in halves(tot[:, near]) + halves(dlt[:, near])]
    scale_parts.append(jnp.zeros((64, 128), f32))
    send3[...] = jnp.concatenate(scale_parts, 0).T[:FAR].astype(bf16)

    for j in range(1, CHIPS):
        there = around(j)
        remote(send3, recv3.at[slot(chip)], s_3, r_3, there * 2 + core).start()
    pltpu.make_async_copy(send3, recv3.at[slot(chip)], r_3).start()
    scaled = []
    for h in range(H):
        rows = pl.ds(W * h, W)
        scaled.append((dat_ref[rows, :].astype(f32) * tot[h : h + 1, :]).astype(bf16))
    dap[...] = jnp.concatenate(scaled, 0).T

    def gather_in(ref, lanes, width, value, fresh):
        if width == 128:
            if fresh:
                ref[:, lanes] = value
            else:
                ref[:, lanes] += value
        else:
            ref[:, pl.ds(lanes.start, 128)] += value[:, :128]
            ref[:, pl.ds(lanes.start + 128, 128)] = value[:, 128:]

    def dscores(h):
        dprob = p0[h].astype(f32) * tot[h : h + 1, :] - dlt[h : h + 1, :]
        return e0[h] * dprob.astype(bf16)

    def backward0(heads):
        dscore = dscores(heads[0])
        for h in heads:
            lanes, rows, width, off = place(h // PER, h % PER)
            value = dot(e0[h], dap[:, lanes] * lane_mask(width, off))
            gather_in(dv, lanes, width, value, h % PER == 0)
            ahead = dscores(h + 1) if h + 1 in heads else None
            p0[h] = dscore
            dqt[rows, :] = dot(kt_ref[rows, :], dscore)
            dscore = ahead

    def backward1(g):
        for p in range(PER // 2):
            lanes, low, high, both, width, off = pair_place(g, p)
            expo = e1[g * (PER // 2) + p]
            a, b = g * PER + 2 * p, g * PER + 2 * p + 1
            scale = jnp.concatenate([tot[a : a + 1, near], tot[b : b + 1, near]], 1)
            delta = jnp.concatenate([dlt[a : a + 1, near], dlt[b : b + 1, near]], 1)
            dprob = p1[g * (PER // 2) + p].astype(f32) * scale - delta
            dscore = expo * dprob.astype(bf16)
            dq = dot(k1t[both, :], dscore)
            dq1t[low, :] = dq[:W, :PAIR]
            dq1t[high, :] = dq[W:, PAIR:]
            value = dot(expo, stacked(dap[near, lanes], off, width))
            gather_in(dv1, lanes, width, value, p == 0)
            value = dot(dscore, stacked(q_ref[near, lanes], off, width))
            gather_in(dk1, lanes, width, value, p == 0)

    def keys0(g):
        for hh in range(PER):
            lanes, rows, width, off = place(g, hh)
            value = dot(p0[g * PER + hh], q_ref[:, lanes] * lane_mask(width, off))
            gather_in(dk, lanes, width, value, hh == 0)

    for g in range(GROUPS):
        backward1(g)
    gsend[0] = dk1[...].astype(bf16)
    gsend[1] = dv1[...].astype(bf16)
    grad_copy = remote(gsend, gback, s_g, r_g, mate)
    grad_copy.start()
    backward0(range(0, 4))

    drain(recv3, r_3)
    scales = recv3[...].astype(f32)
    for_head = (lane & 15) == chip
    far_inv = jnp.sum(jnp.where(for_head & (lane < 32), scales, 0.0), 1, keepdims=True)
    far_del = jnp.sum(jnp.where(for_head & (lane >= 32), scales, 0.0), 1, keepdims=True)
    far_grads = jnp.where(lane >= 64, qda[...].astype(f32) * far_inv, 0.0).astype(bf16)
    far_back = fe[...].astype(f32)
    far_ds = far_back * (dot_nt(far_grads, kv[...] * high) - far_del)
    back_kv = (
        dot(far_ds.T.astype(bf16), qda[...] * low) + dot(far_back.T.astype(bf16), far_grads)
    ).astype(bf16)
    bsame[:, :128] = back_kv[:256]
    bsame[:, 128:] = dot(far_ds.astype(bf16), kv[...] * low).astype(bf16)
    bother[...] = back_kv[256:]
    for j in range(CHIPS):
        there = around(j)
        if j:
            remote(
                bsame.at[slot(there)], rsame.at[slot(chip)], s_4, r_4, there * 2 + core
            ).start()
        remote(
            bother.at[slot(there)], rother.at[slot(chip)], s_5, r_5, there * 2 + (1 - core)
        ).start()
    pltpu.make_async_copy(bsame.at[slot(chip)], rsame.at[slot(chip)], r_4).start()

    backward0(range(4, 16))

    grad_copy.wait()
    drain(rsame, r_4)
    drain(rother, r_5)
    keys_back, values_back, asks_back = [], [], []
    for h in range(H):
        both_back = rsame[pl.ds(h * FAR, FAR)].astype(f32)
        here = both_back[:, :128] + rother[pl.ds(h * FAR, FAR)].astype(f32)
        keys_back.append(here[:, :W])
        values_back.append(here[:, 64 : 64 + W])
        asks_back.append(both_back[:, 128 : 128 + W])
    few = pl.ds(0, FAR)
    dv[near] += gback[1].astype(f32)
    dv[few] += jnp.concatenate(values_back, 1)
    dqt[:, near] += dq1t[...]
    gq = (dqt[...] * SHARP).astype(bf16).T
    first_rows = dqt[:, near].T[:FAR] + jnp.concatenate(asks_back, 1)
    gq = jnp.concatenate([(first_rows * SHARP).astype(bf16), gq[FAR:]], 0)
    gv = dv[...].astype(bf16)
    back = dot_nt(gq, uq) + dot_nt(gv, uv)
    back_both = jnp.concatenate(halves(back), 1)
    bu, bl = halves(back.T[: 2 * R])
    lu, ll = halves(lift_s[...])
    from_back = dot(jnp.concatenate([bu, bl], 0), normed_s[...])
    from_back = 2.0 * (from_back[:16] + from_back[16:])
    lifts = jnp.concatenate([lu, ll], 0)
    from_q = dot(lifts, gq)
    from_q = 2.0 * (from_q[:R] + from_q[16 : 16 + R])
    from_v = dot(lifts, gv)
    from_v = 2.0 * (from_v[R:16] + from_v[16 + R : 32])
    pairs = [
        jnp.concatenate([from_back[:R], from_q], 0), jnp.concatenate([from_back[R:16], from_v], 0)
    ]
    for p in range(2):
        for c in range(6):
            part[p * 6 + c] = pairs[p][:, 128 * c : 128 * c + 128].astype(bf16)

    def first(j, carry):
        there = lax.rem(mine + j, 16)

        @pl.when(there < SLICES)
        def _():
            remote_to(part.at[there], one.at[mine], s_6, r_6, plane_peer(j)).start()

        return carry

    lax.fori_loop(1, 16, first, 0)

    @pl.when(mine < SLICES)
    def _():
        pltpu.make_async_copy(part.at[mine], one.at[mine], r_6).start()

    for g in range(GROUPS):
        keys0(g)

    @pl.when(mine < SLICES)
    def _():
        drain(one, r_6)
        total[0] = jnp.sum(one[...].astype(f32), 0).astype(bf16)

        for j in range(1, 16):
            remote_to(total.at[0], two.at[column], s_7, r_7, column_peer(j)).start()
        pltpu.make_async_copy(total.at[0], two.at[column], r_7).start()

    dk[near] += gback[0].astype(f32)
    dk[few] += jnp.concatenate(keys_back, 1)
    gk = (dk[...] * LN2).astype(bf16)
    grad = (
        dot_nt(gq, wq_ref[...])
        + dot_nt(gk, wk_ref[...])
        + dot_nt(gv, wv_ref[...])
        + 2.0 * dot(back_both, jnp.concatenate([down, down], 0))
    )
    s = grad * gain_ref[...].astype(f32)

    @pl.when(mine < SLICES)
    def _():
        drain(two, r_7)
        both_sum = jnp.sum(two[...].astype(f32), 0) * (1.0 / math.sqrt(SEQ * DP * T))
        total[1] = both_sum.astype(bf16)

        for j in range(1, 16):
            remote_to(total.at[1], done.at[mine], s_8, r_8, plane_peer(j)).start()
        pltpu.make_async_copy(total.at[1], done.at[mine], r_8).start()

    xhat = xhat_s[...]
    out = scale_s[:, 0:1] * (
        s - jnp.mean(s, -1, keepdims=True) - xhat * jnp.mean(s * xhat, -1, keepdims=True)
    )
    unorder = jnp.where(place_of(iota((1, T), 1)) == iota((T, T), 0), 1.0, 0.0).astype(bf16)
    out_s[0] = dot(unorder, out.astype(bf16)).astype(bf16)
    leave = pltpu.make_async_copy(out_s, out_ref, s_out)
    leave.start()
    drain(done, r_8)
    for p in range(2):
        for c in range(6):
            tile = done[p * 6 + c].astype(f32)
            merged_ref[2 * p, :, 128 * c : 128 * c + 128] = tile[:R]
            merged_ref[2 * p + 1, :, 128 * c : 128 * c + 128] = tile[R:]

    leave.wait()
    drain(same.at[pl.ds(0, (CHIPS - 1) * FAR)], s_kv)
    drain(other, s_qd)
    drain(recv2.at[pl.ds(0, (CHIPS - 1) * FAR)], s_2)
    drain(recv3.at[pl.ds(0, (CHIPS - 1) * FAR)], s_3)
    drain(rsame.at[pl.ds(0, (CHIPS - 1) * FAR)], s_4)
    drain(rother, s_5)

    @pl.when(mine < SLICES)
    def _():
        drain(one.at[pl.ds(0, SLICES - 1)], s_6)
        drain(two.at[pl.ds(0, 15)], s_7)
        drain(one.at[pl.ds(0, 15)], s_8)

    @pl.when(mine >= SLICES)
    def _():
        drain(one.at[pl.ds(0, SLICES)], s_6)


def hand_on_kernel(out_in, merged_in, out_ref, merged_ref, sems):
    copies = [
        pltpu.make_async_copy(out_in, out_ref, sems.at[0]),
        pltpu.make_async_copy(merged_in, merged_ref, sems.at[1]),
    ]
    for copy in copies:
        copy.start()
    for copy in copies:
        copy.wait()


def shape(*dims, kind=bf16):
    return jax.ShapeDtypeStruct(dims, kind)


def whole():
    return pl.BlockSpec(memory_space=pltpu.VMEM)


def far():
    return pl.BlockSpec(memory_space=pl.ANY)


def per_device(
    tiles, cotangent, gain, query_matrix, key_matrix, value_matrix, w_out,
    query_down_factor, query_up_factor, value_down_factor, value_up_factor, valid_count,
):
    buf = pltpu.VMEM
    sem = pltpu.SemaphoreType.DMA
    out, merged = pl.pallas_call(
        layer_kernel,
        out_shape=[shape(1, T, D), shape(4, R, D, kind=f32)],
        in_specs=[pl.BlockSpec(memory_space=pltpu.SMEM), whole(), far(), whole()] + [far()] * 4
        + [whole()] * 4,
        out_specs=[far(), whole()],
        scratch_shapes=[
            buf((1, T, D), bf16), buf((D, D), bf16), buf((D, D), bf16), buf((D, D), bf16),
            buf((D, D), bf16), sem((5,)), buf((1, T, D), bf16), sem,
            buf((T, D), f32), buf((T, 128), f32), buf((T, D), bf16), buf((2 * R, T), f32),
            buf((T, D), bf16), buf((T, D), bf16), buf((T, D), bf16),
            buf((D, T), bf16), buf((D, T), bf16), buf((D, T), bf16),
            buf((H, FAR, 256), bf16),
            buf((H, T, T), bf16), buf((H, T, T), bf16),
            buf((H // 2, PAIR, 256), bf16), buf((H // 2, PAIR, 256), bf16),
            buf((T, T), bf16), buf((PAIR, 256), bf16),
            buf((H, T), f32), buf((H, T), f32), buf((H, T), f32),
            buf((T, D), bf16), buf((D, T), f32), buf((D, PAIR), f32),
            buf((T, D), f32), buf((T, D), f32),
            buf((PAIR, D), bf16), buf((PAIR, D), bf16), buf((D, PAIR), bf16),
            buf((PAIR, D), f32), buf((PAIR, D), f32),
            buf((2, PAIR, D), bf16), buf((2, PAIR, D), bf16),
            buf((256, 256), bf16), buf((256, 128), bf16),
            buf((T, 128), bf16), buf((256, 128), bf16), buf((256, T), bf16),
            buf((256, 128), bf16), buf((256, 128), bf16),
            buf((FAR, 128), bf16), buf((256, 128), bf16),
            buf((256, 256), bf16), buf((256, 128), bf16),
            buf((256, 256), bf16), buf((256, 128), bf16),
            buf((SLICES, 16, 128), bf16), buf((16, 16, 128), bf16), buf((2, 16, 128), bf16),
            buf((16, 16, 128), bf16), buf((SLICES, 16, 128), bf16),
            sem, sem, sem, sem, sem((3,)), sem((3,)), sem, sem, sem, sem, sem, sem, sem, sem,
            sem, sem, sem, sem, sem, sem, sem, sem,
        ],
        compiler_params=pltpu.CompilerParams(
            vmem_limit_bytes=VMEM_LIMIT, collective_id=0, has_side_effects=True
        ),
        name="layer",
    )(
        valid_count, tiles, cotangent, gain, query_matrix, key_matrix, value_matrix, w_out,
        query_down_factor.T, query_up_factor, value_down_factor.T, value_up_factor,
    )
    return pl.pallas_call(
        hand_on_kernel,
        out_shape=[shape(1, T, D), shape(4, R, D, kind=f32)],
        in_specs=[whole()] * 2,
        out_specs=[far()] * 2,
        scratch_shapes=[sem((2,))],
        name="hand_on",
    )(out, merged)


def solution(mesh):
    placed = (P("dp", "seq", None),) * 2 + (P(),) * 9 + (P("dp"),)
    return jax.shard_map(
        per_device,
        mesh=mesh,
        in_specs=placed,
        out_specs=(P("dp", "seq", None), P()),
        check_vma=False,
    )
```

```python
import math

import jax
import jax.numpy as jnp
from jax import lax
from jax.experimental import pallas as pl
from jax.experimental.pallas import tpu as pltpu
from jax.sharding import PartitionSpec as P

T = 512
D = 768
H = 16
W = 48
R = 8
PAIR = 128
FAR = 16
SEQ = 32
DP = 8
CHIPS = 16
GROUPS = 2
SLICES = 12
PER = 8
EPS = 1e-5
LOG2E = math.log2(math.e)
SHARP = 1.0 / math.sqrt(W)
LN2 = math.log(2.0)
MESH = pl.DeviceIdType.MESH
f32 = jnp.float32
bf16 = jnp.bfloat16
VMEM_LIMIT = 56 * 1024 * 1024


def iota(shape, axis):
    return lax.broadcasted_iota(jnp.int32, shape, axis)


def dot(a, b):
    return jnp.dot(a, b, preferred_element_type=f32)


def dot_nt(a, b):
    return lax.dot_general(a, b, (((1,), (1,)), ((), ())), preferred_element_type=f32)


def place_of(row):
    return (row & 15) * 32 + ((row >> 4) & 7) * 4 + (row >> 7)


def order_matrix(first, count):
    place = place_of(first + iota((count, 128), 0))
    lane = iota((count, 128), 1)
    parts = [jnp.where(place == lane + 128 * c, 1.0, 0.0) for c in range(4)]
    return jnp.concatenate(parts, 1).astype(bf16)


def halves(value):
    upper = value.astype(bf16)
    lower = (value - upper.astype(f32)).astype(bf16)
    return upper, lower


def normalize(x):
    center = x - jnp.mean(x, -1, keepdims=True)
    inverse = lax.rsqrt(jnp.mean(center * center, -1, keepdims=True) + EPS)
    return center * inverse, inverse


def window(hh):
    low = W * hh
    first = low // 128
    last = (low + W - 1) // 128
    return first * 128, (last - first + 1) * 128, low - first * 128


def pair_window(p):
    low = 2 * W * p
    first = low // 128
    last = (low + 2 * W - 1) // 128
    return first * 128, (last - first + 1) * 128, low - first * 128


def lane_mask(width, off):
    lane = iota((1, width), 1)
    return jnp.where((lane >= off) & (lane < off + W), 1.0, 0.0).astype(bf16)


def pad_rows(block, off, width):
    parts = []
    if off:
        parts.append(jnp.zeros((off, block.shape[1]), block.dtype))
    parts.append(block)
    rest = width - off - block.shape[0]
    if rest:
        parts.append(jnp.zeros((rest, block.shape[1]), block.dtype))
    return jnp.concatenate(parts, 0)


def down_rows(qd_ref, vd_ref):
    return jnp.concatenate(
        [qd_ref[...].astype(f32), vd_ref[...].astype(f32), jnp.zeros((112, D), f32)], 0
    ).astype(bf16)


def up_padded(u_ref, at):
    return pad_rows(u_ref[...].astype(f32), at, 128).astype(bf16)


def layer_kernel(
    valid_ref, tiles_ref, cot_hbm, gain_ref, wq_hbm, wk_hbm, wv_hbm, wo_hbm,
    qd_ref, qu_ref, vd_ref, vu_ref,
    out_ref, merged_ref,
    cot_ref, wq_ref, wk_ref, wv_ref, wo_ref, s_in, out_s, s_out,
    xhat_s, scale_s, normed_s, lift_s, q_ref, k_ref, v_ref, qt_ref, kt_ref, dat_ref,
    sfar,
    e0, p0, e1, p1, mask0, mask1, tot, rsum, dlt, dap, dqt, dq1t, dk, dv,
    k1, v1, k1t, dk1, dv1, gsend, gback,
    same, other, kv, qda, fe, send2, recv2, send3, recv3, bsame, bother, rsame, rother,
    part, one, total, two, done,
    s_kv, r_kv, s_qd, r_qd, s_pair, r_pair, s_2, r_2, s_3, r_3, s_4, r_4, s_5, r_5, s_g, r_g,
    s_6, r_6, s_7, r_7, s_8, r_8,
):
    dp = lax.axis_index("dp")
    me = lax.axis_index("seq")
    chip = lax.div(me, 2)
    core = lax.rem(me, 2)
    mate = chip * 2 + (1 - core)
    column = lax.rem(me, 16)
    half = lax.div(me, 16)
    mine = dp * 2 + half
    valid = valid_ref[0]

    def plane_peer(j):
        there = lax.rem(mine + j, 16)
        return {"dp": lax.div(there, 2), "seq": lax.rem(there, 2) * 16 + column}

    def column_peer(j):
        return {"seq": half * 16 + lax.rem(column + j, 16)}

    barrier = pltpu.get_barrier_semaphore()

    for j in range(1, SEQ):
        pl.semaphore_signal(
            barrier, inc=1, device_id={"seq": lax.rem(me + j, SEQ)}, device_id_type=MESH
        )
    for j in range(1, 16):
        pl.semaphore_signal(barrier, inc=1, device_id=plane_peer(j), device_id_type=MESH)

    def remote_to(src, dst, send, recv, peer):
        return pltpu.make_async_remote_copy(
            src_ref=src, dst_ref=dst, send_sem=send, recv_sem=recv,
            device_id=peer, device_id_type=MESH,
        )

    def remote(src, dst, send, recv, peer):
        return remote_to(src, dst, send, recv, {"seq": peer})

    def drain(ref, sem):
        pltpu.make_async_copy(ref, ref, sem).wait()

    loads = [
        pltpu.make_async_copy(src, dst, s_in.at[i])
        for i, (src, dst) in enumerate(
            [(cot_hbm, cot_ref), (wo_hbm, wo_ref), (wq_hbm, wq_ref), (wk_hbm, wk_ref), (wv_hbm, wv_ref)]
        )
    ]
    for load in loads:
        load.start()

    down = down_rows(qd_ref, vd_ref)
    uq = up_padded(qu_ref, 0)
    uv = up_padded(vu_ref, R)

    def project(first, count, arrive):
        some = pl.ds(first, count)
        order = order_matrix(first, count)
        x = dot(order, tiles_ref[0])
        arrive(0, 1)
        cot = dot(order, cot_ref[0]).astype(bf16)
        da = dot_nt(cot, wo_ref[...]).astype(bf16)
        dat_ref[:, some] = da.T
        xhat, inverse_dev = normalize(x)
        xhat_s[some] = xhat
        scale_s[some] = jnp.broadcast_to(inverse_dev, (count, 128))
        normed = (xhat * gain_ref[...].astype(f32)).astype(bf16)
        normed_s[some] = normed
        lift = dot_nt(normed, down)
        both = jnp.concatenate(halves(lift), 1)
        lift_s[:, some] = lift.T[: 2 * R]
        arrive(2, 3, 4)
        q = dot(normed, wq_ref[...]) + 2.0 * dot(both, jnp.concatenate([uq, uq], 0))
        q = (q * (SHARP * LOG2E)).astype(bf16)
        q_ref[some] = q
        qt_ref[:, some] = q.T
        k = dot(normed, wk_ref[...]).astype(bf16)
        k_ref[some] = k
        kt_ref[:, some] = k.T
        v = (dot(normed, wv_ref[...]) + 2.0 * dot(both, jnp.concatenate([uv, uv], 0))).astype(bf16)
        v_ref[some] = v
        return q, k, v, da

    def arrive(*which):
        for i in which:
            loads[i].wait()

    q, k, v, da = project(0, PAIR, arrive)
    gap = jnp.zeros((FAR, 64 - W), f32)
    qf, kf, vf, df = (rows[:FAR].astype(f32) for rows in (q, k, v, da))
    for h in range(H):
        cut = slice(W * h, W * h + W)
        four = [kf[:, cut], gap, vf[:, cut], gap, qf[:, cut], gap, df[:, cut], gap]
        sfar[h] = jnp.concatenate(four, 1).astype(bf16)

    pl.semaphore_wait(barrier, SEQ - 1 + 15)

    def slot(c):
        return pl.ds(pl.multiple_of(c * FAR, FAR), FAR)

    def around(j):
        return lax.rem(chip + j, CHIPS)

    for j in range(CHIPS):
        there = around(j)
        if j:
            remote(sfar.at[there], same.at[slot(chip)], s_kv, r_kv, there * 2 + core).start()
        keys_only = sfar.at[there, :, pl.ds(0, 128)]
        remote(keys_only, other.at[slot(chip)], s_qd, r_qd, there * 2 + (1 - core)).start()
    pltpu.make_async_copy(sfar.at[chip], same.at[slot(chip)], r_kv).start()

    near = pl.ds(0, PAIR)
    pair_copies = [
        remote(k_ref.at[near], k1, s_pair.at[0], r_pair.at[0], mate),
        remote(v_ref.at[near], v1, s_pair.at[1], r_pair.at[1], mate),
        remote(kt_ref.at[:, near], k1t, s_pair.at[2], r_pair.at[2], mate),
    ]
    for copy in pair_copies:
        copy.start()

    project(PAIR, T - PAIR, lambda *which: None)

    row = iota((T, 128), 0)
    col = iota((T, 128), 1)
    seen = me * T + place_of(row) < valid
    for c in range(4):
        open0 = seen | (row == col + 128 * c)
        mask0[:, 128 * c : 128 * c + 128] = jnp.where(open0, jnp.inf, 0.0).astype(bf16)
    row = iota((PAIR, 2 * PAIR), 0)
    mask1[...] = jnp.where(mate * T + place_of(row) < valid, jnp.inf, 0.0).astype(bf16)

    def place(g, hh):
        base, width, off = window(hh)
        return pl.ds(g * 384 + base, width), pl.ds(g * 384 + W * hh, W), width, off

    def eight(g):
        return pl.ds(pl.multiple_of(g * PER, PER), PER)

    def column_sums(expo, dprob):
        expo = expo.astype(f32)
        return jnp.sum(expo, 0, keepdims=True), jnp.sum(expo * dprob, 0, keepdims=True)

    def forward0(heads):
        def operands(h, c):
            lanes, rows, width, off = place(h // PER, h % PER)
            cols = pl.ds(256 * c, 256)
            return (
                lanes, pad_rows(qt_ref[rows, cols], off, width),
                pad_rows(dat_ref[rows, cols], off, width),
            )

        def products(given, b):
            lanes, ask, grad = given
            block = pl.ds(128 * b, 128)
            return dot(k_ref[block, lanes], ask), dot(v_ref[block, lanes], grad)

        def fold(value):
            return jnp.sum(value.reshape(16, 8, 256), 0)

        steps = [(h, c, b) for h in heads for c in range(2) for b in range(4)]
        given = operands(heads[0], 0)
        score, dprob = products(given, 0)
        total = mixed = None
        for n, (h, c, b) in enumerate(steps):
            ahead = (None, None)
            if n + 1 < len(steps):
                after = steps[n + 1]
                if after[2] == 0:
                    given = operands(after[0], after[1])
                ahead = products(given, after[2])
            block = pl.ds(128 * b, 128)
            cols = pl.ds(256 * c, 256)
            expo = jnp.minimum(jnp.exp2(score).astype(bf16), mask0[block, cols])
            if c == 0 and b == 0:
                corner = expo[:, :PAIR]
                expo = jnp.concatenate([corner + corner, expo[:, PAIR:]], 1)
            e0[h, block, cols] = expo
            p0[h, block, cols] = dprob.astype(bf16)
            wide = expo.astype(f32)
            if b == 0:
                total, mixed = fold(wide), fold(wide * dprob)
            else:
                total, mixed = total + fold(wide), mixed + fold(wide * dprob)
            if b == 3:
                tot[h : h + 1, cols] = jnp.sum(total, 0, keepdims=True)
                rsum[h : h + 1, cols] = jnp.sum(mixed, 0, keepdims=True)
            score, dprob = ahead

    def pair_place(g, p):
        base, width, off = pair_window(p)
        lanes = pl.ds(g * 384 + base, width)
        low = pl.ds(pl.multiple_of(g * 384 + 2 * W * p, 16), W)
        high = pl.ds(pl.multiple_of(g * 384 + 2 * W * p + W, 16), W)
        both = pl.ds(pl.multiple_of(g * 384 + 2 * W * p, 16), 2 * W)
        return lanes, low, high, both, width, off

    def side_by_side(low, high, off, width):
        none = jnp.zeros((W, PAIR), bf16)
        block = jnp.concatenate(
            [jnp.concatenate([low, none], 1), jnp.concatenate([none, high], 1)], 0
        )
        return pad_rows(block, off, width)

    def stacked(rows, off, width):
        return jnp.concatenate([rows * lane_mask(width, off), rows * lane_mask(width, off + W)], 0)

    def forward1(g):
        totals, sums = [], []
        for p in range(PER // 2):
            lanes, low, high, both, width, off = pair_place(g, p)
            ask = side_by_side(qt_ref[low, near], qt_ref[high, near], off, width)
            given = side_by_side(dat_ref[low, near], dat_ref[high, near], off, width)
            expo = jnp.minimum(jnp.exp2(dot(k1[:, lanes], ask)).astype(bf16), mask1[...])
            dprob = dot(v1[:, lanes], given)
            e1[g * (PER // 2) + p] = expo
            p1[g * (PER // 2) + p] = dprob.astype(bf16)
            here, mixed = column_sums(expo, dprob)
            totals += [here[:, :PAIR], here[:, PAIR:]]
            sums += [mixed[:, :PAIR], mixed[:, PAIR:]]
        tot[eight(g), near] += jnp.concatenate(totals, 0)
        rsum[eight(g), near] += jnp.concatenate(sums, 0)

    forward0(range(0, 6))

    drain(same, r_kv)
    drain(other, r_qd)
    kv[pl.ds(0, 256)] = same[:, :128]
    kv[pl.ds(256, 256)] = other[...]
    qda[...] = same[:, 128:]
    lane = iota((1, 128), 1)
    low = jnp.where(lane < 64, 1.0, 0.0).astype(bf16)
    high = jnp.where(lane >= 64, 1.0, 0.0).astype(bf16)
    i2 = iota((256, T), 0)
    j2 = iota((1, T), 1)
    j2_core = (j2 >> 8) * (1 - core) + (1 - (j2 >> 8)) * core
    j2_pos = (((j2 & 255) >> 4) * 2 + j2_core) * T + (j2 & 15) * 32
    open2 = (j2_pos < valid) | (j2 == i2)
    far_expo = jnp.exp2(dot_nt(qda[...], kv[...] * low))
    far_expo = jnp.where(open2, far_expo, 0.0).astype(bf16)
    fe[...] = far_expo
    first_lane = jnp.where(lane == 0, 1.0, 0.0).astype(bf16)
    far_mixed = dot(far_expo, kv[...] * high + first_lane)
    far_r = jnp.sum(
        jnp.where(lane >= 64, qda[...].astype(f32) * far_mixed, 0.0), 1, keepdims=True
    )
    far_t = far_mixed[:, 0:1]
    far_parts = halves(far_t) + halves(far_r)
    packed = jnp.zeros((256, 128), f32)
    for i in range(4):
        packed = packed + jnp.where(lane == 16 * i + chip, far_parts[i].astype(f32), 0.0)
    send2[...] = packed.astype(bf16)

    for j in range(1, CHIPS):
        there = around(j)
        remote(send2.at[slot(there)], recv2.at[slot(chip)], s_2, r_2, there * 2 + core).start()
    pltpu.make_async_copy(send2.at[slot(chip)], recv2.at[slot(chip)], r_2).start()

    forward0(range(6, 16))
    for copy in pair_copies:
        copy.wait()
    for g in range(GROUPS):
        forward1(g)

    wide = pl.ds(PAIR, T - PAIR)

    def settle(cols):
        inverse = 1.0 / tot[:, cols]
        tot[:, cols] = inverse
        dlt[:, cols] = rsum[:, cols] * inverse * inverse

    def scale_grads(cols):
        scaled = []
        for h in range(H):
            part_t = dat_ref[pl.ds(W * h, W), cols].astype(f32)
            scaled.append((part_t * tot[h : h + 1, cols]).astype(bf16))
        dap[cols] = jnp.concatenate(scaled, 0).T

    settle(wide)
    scale_grads(wide)
    drain(recv2, r_2)
    gathered = recv2[pl.ds(0, FAR)].astype(f32)
    for c in range(1, CHIPS):
        gathered = gathered + recv2[pl.ds(c * FAR, FAR)].astype(f32)
    turned = jnp.concatenate([gathered, jnp.zeros((PAIR - FAR, 128), f32)], 0).T
    tot[:, near] += turned[:16] + turned[16:32]
    rsum[:, near] += turned[32:48] + turned[48:64]
    settle(near)
    scale_parts = [part.astype(f32) for part in halves(tot[:, near]) + halves(dlt[:, near])]
    scale_parts.append(jnp.zeros((64, 128), f32))
    send3[...] = jnp.concatenate(scale_parts, 0).T[:FAR].astype(bf16)

    for j in range(1, CHIPS):
        there = around(j)
        remote(send3, recv3.at[slot(chip)], s_3, r_3, there * 2 + core).start()
    pltpu.make_async_copy(send3, recv3.at[slot(chip)], r_3).start()
    scale_grads(near)

    def gather_in(ref, lanes, width, value, fresh):
        if width == 128:
            if fresh:
                ref[:, lanes] = value
            else:
                ref[:, lanes] += value
        else:
            ref[:, pl.ds(lanes.start, 128)] += value[:, :128]
            ref[:, pl.ds(lanes.start + 128, 128)] = value[:, 128:]

    def dscores(h):
        dprob = p0[h].astype(f32) * tot[h : h + 1, :] - dlt[h : h + 1, :]
        return e0[h] * dprob.astype(bf16)

    def backward0(heads):
        dscore = dscores(heads[0])
        for h in heads:
            lanes, rows, width, off = place(h // PER, h % PER)
            value = dot(e0[h], dap[:, lanes] * lane_mask(width, off))
            gather_in(dv, lanes, width, value, h % PER == 0)
            ahead = dscores(h + 1) if h + 1 in heads else None
            p0[h] = dscore
            dqt[rows, :] = dot(kt_ref[rows, :], dscore)
            dscore = ahead

    def backward1(g):
        for p in range(PER // 2):
            lanes, low, high, both, width, off = pair_place(g, p)
            expo = e1[g * (PER // 2) + p]
            a, b = g * PER + 2 * p, g * PER + 2 * p + 1
            scale = jnp.concatenate([tot[a : a + 1, near], tot[b : b + 1, near]], 1)
            delta = jnp.concatenate([dlt[a : a + 1, near], dlt[b : b + 1, near]], 1)
            dprob = p1[g * (PER // 2) + p].astype(f32) * scale - delta
            dscore = expo * dprob.astype(bf16)
            dq = dot(k1t[both, :], dscore)
            dq1t[low, :] = dq[:W, :PAIR]
            dq1t[high, :] = dq[W:, PAIR:]
            value = dot(expo, stacked(dap[near, lanes], off, width))
            gather_in(dv1, lanes, width, value, p == 0)
            value = dot(dscore, stacked(q_ref[near, lanes], off, width))
            gather_in(dk1, lanes, width, value, p == 0)

    def keys0(g):
        for hh in range(PER):
            lanes, rows, width, off = place(g, hh)
            value = dot(p0[g * PER + hh], q_ref[:, lanes] * lane_mask(width, off))
            gather_in(dk, lanes, width, value, hh == 0)

    for g in range(GROUPS):
        backward1(g)
    gsend[0] = dk1[...].astype(bf16)
    gsend[1] = dv1[...].astype(bf16)
    grad_copy = remote(gsend, gback, s_g, r_g, mate)
    grad_copy.start()
    backward0(range(0, 4))

    drain(recv3, r_3)
    scales = recv3[...].astype(f32)
    for_head = (lane & 15) == chip
    far_inv = jnp.sum(jnp.where(for_head & (lane < 32), scales, 0.0), 1, keepdims=True)
    far_del = jnp.sum(jnp.where(for_head & (lane >= 32), scales, 0.0), 1, keepdims=True)
    far_grads = jnp.where(lane >= 64, qda[...].astype(f32) * far_inv, 0.0).astype(bf16)
    far_back = fe[...].astype(f32)
    far_ds = far_back * (dot_nt(far_grads, kv[...] * high) - far_del)
    back_kv = (
        dot(far_ds.T.astype(bf16), qda[...] * low) + dot(far_back.T.astype(bf16), far_grads)
    ).astype(bf16)
    bsame[:, :128] = back_kv[:256]
    bsame[:, 128:] = dot(far_ds.astype(bf16), kv[...] * low).astype(bf16)
    bother[...] = back_kv[256:]
    for j in range(CHIPS):
        there = around(j)
        if j:
            remote(
                bsame.at[slot(there)], rsame.at[slot(chip)], s_4, r_4, there * 2 + core
            ).start()
        remote(
            bother.at[slot(there)], rother.at[slot(chip)], s_5, r_5, there * 2 + (1 - core)
        ).start()
    pltpu.make_async_copy(bsame.at[slot(chip)], rsame.at[slot(chip)], r_4).start()

    backward0(range(4, 16))

    grad_copy.wait()
    dv[near] += gback[1].astype(f32)
    dqt[:, near] += dq1t[...]
    gq_rest = (dqt[...] * SHARP).astype(bf16).T
    gq_first = dqt[:, near].T[:FAR]
    lu, ll = halves(lift_s[...])
    drain(rsame, r_4)
    drain(rother, r_5)
    keys_back, values_back, asks_back = [], [], []
    for h in range(H):
        both_back = rsame[pl.ds(h * FAR, FAR)].astype(f32)
        here = both_back[:, :128] + rother[pl.ds(h * FAR, FAR)].astype(f32)
        keys_back.append(here[:, :W])
        values_back.append(here[:, 64 : 64 + W])
        asks_back.append(both_back[:, 128 : 128 + W])
    few = pl.ds(0, FAR)
    dv[few] += jnp.concatenate(values_back, 1)
    first_rows = gq_first + jnp.concatenate(asks_back, 1)
    gq = jnp.concatenate([(first_rows * SHARP).astype(bf16), gq_rest[FAR:]], 0)
    gv = dv[...].astype(bf16)
    back = dot_nt(gq, uq) + dot_nt(gv, uv)
    back_both = jnp.concatenate(halves(back), 1)
    bu, bl = halves(back.T[: 2 * R])
    from_back = dot(jnp.concatenate([bu, bl], 0), normed_s[...])
    from_back = 2.0 * (from_back[:16] + from_back[16:])
    lifts = jnp.concatenate([lu, ll], 0)
    from_q = dot(lifts, gq)
    from_q = 2.0 * (from_q[:R] + from_q[16 : 16 + R])
    from_v = dot(lifts, gv)
    from_v = 2.0 * (from_v[R:16] + from_v[16 + R : 32])
    pairs = [
        jnp.concatenate([from_back[:R], from_q], 0), jnp.concatenate([from_back[R:16], from_v], 0)
    ]
    for p in range(2):
        for c in range(6):
            part[p * 6 + c] = pairs[p][:, 128 * c : 128 * c + 128].astype(bf16)

    def first(j, carry):
        there = lax.rem(mine + j, 16)

        @pl.when(there < SLICES)
        def _():
            remote_to(part.at[there], one.at[mine], s_6, r_6, plane_peer(j)).start()

        return carry

    lax.fori_loop(1, 16, first, 0)

    @pl.when(mine < SLICES)
    def _():
        pltpu.make_async_copy(part.at[mine], one.at[mine], r_6).start()

    for g in range(GROUPS):
        keys0(g)

    @pl.when(mine < SLICES)
    def _():
        drain(one, r_6)
        total[0] = jnp.sum(one[...].astype(f32), 0).astype(bf16)

        for j in range(1, 16):
            remote_to(total.at[0], two.at[column], s_7, r_7, column_peer(j)).start()
        pltpu.make_async_copy(total.at[0], two.at[column], r_7).start()

    dk[near] += gback[0].astype(f32)
    dk[few] += jnp.concatenate(keys_back, 1)
    gk = (dk[...] * LN2).astype(bf16)
    grad = (
        dot_nt(gq, wq_ref[...])
        + dot_nt(gk, wk_ref[...])
        + dot_nt(gv, wv_ref[...])
        + 2.0 * dot(back_both, jnp.concatenate([down, down], 0))
    )
    s = grad * gain_ref[...].astype(f32)

    @pl.when(mine < SLICES)
    def _():
        drain(two, r_7)
        both_sum = jnp.sum(two[...].astype(f32), 0) * (1.0 / math.sqrt(SEQ * DP * T))
        total[1] = both_sum.astype(bf16)

        for j in range(1, 16):
            remote_to(total.at[1], done.at[mine], s_8, r_8, plane_peer(j)).start()
        pltpu.make_async_copy(total.at[1], done.at[mine], r_8).start()

    xhat = xhat_s[...]
    out = scale_s[:, 0:1] * (
        s - jnp.mean(s, -1, keepdims=True) - xhat * jnp.mean(s * xhat, -1, keepdims=True)
    )
    unorder = jnp.where(place_of(iota((1, T), 1)) == iota((T, T), 0), 1.0, 0.0).astype(bf16)
    out_s[0] = dot(unorder, out.astype(bf16)).astype(bf16)
    leave = pltpu.make_async_copy(out_s, out_ref, s_out)
    leave.start()
    drain(done, r_8)
    for p in range(2):
        for c in range(6):
            tile = done[p * 6 + c].astype(f32)
            merged_ref[2 * p, :, 128 * c : 128 * c + 128] = tile[:R]
            merged_ref[2 * p + 1, :, 128 * c : 128 * c + 128] = tile[R:]

    leave.wait()
    drain(same.at[pl.ds(0, (CHIPS - 1) * FAR)], s_kv)
    drain(other, s_qd)
    drain(recv2.at[pl.ds(0, (CHIPS - 1) * FAR)], s_2)
    drain(recv3.at[pl.ds(0, (CHIPS - 1) * FAR)], s_3)
    drain(rsame.at[pl.ds(0, (CHIPS - 1) * FAR)], s_4)
    drain(rother, s_5)

    @pl.when(mine < SLICES)
    def _():
        drain(one.at[pl.ds(0, SLICES - 1)], s_6)
        drain(two.at[pl.ds(0, 15)], s_7)
        drain(one.at[pl.ds(0, 15)], s_8)

    @pl.when(mine >= SLICES)
    def _():
        drain(one.at[pl.ds(0, SLICES)], s_6)


def hand_on_kernel(out_in, merged_in, out_ref, merged_ref, sems):
    copies = [
        pltpu.make_async_copy(out_in, out_ref, sems.at[0]),
        pltpu.make_async_copy(merged_in, merged_ref, sems.at[1]),
    ]
    for copy in copies:
        copy.start()
    for copy in copies:
        copy.wait()


def shape(*dims, kind=bf16):
    return jax.ShapeDtypeStruct(dims, kind)


def whole():
    return pl.BlockSpec(memory_space=pltpu.VMEM)


def far():
    return pl.BlockSpec(memory_space=pl.ANY)


def per_device(
    tiles, cotangent, gain, query_matrix, key_matrix, value_matrix, w_out,
    query_down_factor, query_up_factor, value_down_factor, value_up_factor, valid_count,
):
    buf = pltpu.VMEM
    sem = pltpu.SemaphoreType.DMA
    out, merged = pl.pallas_call(
        layer_kernel,
        out_shape=[shape(1, T, D), shape(4, R, D, kind=f32)],
        in_specs=[pl.BlockSpec(memory_space=pltpu.SMEM), whole(), far(), whole()] + [far()] * 4
        + [whole()] * 4,
        out_specs=[far(), whole()],
        scratch_shapes=[
            buf((1, T, D), bf16), buf((D, D), bf16), buf((D, D), bf16), buf((D, D), bf16),
            buf((D, D), bf16), sem((5,)), buf((1, T, D), bf16), sem,
            buf((T, D), f32), buf((T, 128), f32), buf((T, D), bf16), buf((2 * R, T), f32),
            buf((T, D), bf16), buf((T, D), bf16), buf((T, D), bf16),
            buf((D, T), bf16), buf((D, T), bf16), buf((D, T), bf16),
            buf((H, FAR, 256), bf16),
            buf((H, T, T), bf16), buf((H, T, T), bf16),
            buf((H // 2, PAIR, 256), bf16), buf((H // 2, PAIR, 256), bf16),
            buf((T, T), bf16), buf((PAIR, 256), bf16),
            buf((H, T), f32), buf((H, T), f32), buf((H, T), f32),
            buf((T, D), bf16), buf((D, T), f32), buf((D, PAIR), f32),
            buf((T, D), f32), buf((T, D), f32),
            buf((PAIR, D), bf16), buf((PAIR, D), bf16), buf((D, PAIR), bf16),
            buf((PAIR, D), f32), buf((PAIR, D), f32),
            buf((2, PAIR, D), bf16), buf((2, PAIR, D), bf16),
            buf((256, 256), bf16), buf((256, 128), bf16),
            buf((T, 128), bf16), buf((256, 128), bf16), buf((256, T), bf16),
            buf((256, 128), bf16), buf((256, 128), bf16),
            buf((FAR, 128), bf16), buf((256, 128), bf16),
            buf((256, 256), bf16), buf((256, 128), bf16),
            buf((256, 256), bf16), buf((256, 128), bf16),
            buf((SLICES, 16, 128), bf16), buf((16, 16, 128), bf16), buf((2, 16, 128), bf16),
            buf((16, 16, 128), bf16), buf((SLICES, 16, 128), bf16),
            sem, sem, sem, sem, sem((3,)), sem((3,)), sem, sem, sem, sem, sem, sem, sem, sem,
            sem, sem, sem, sem, sem, sem, sem, sem,
        ],
        compiler_params=pltpu.CompilerParams(
            vmem_limit_bytes=VMEM_LIMIT, collective_id=0, has_side_effects=True
        ),
        name="layer",
    )(
        valid_count, tiles, cotangent, gain, query_matrix, key_matrix, value_matrix, w_out,
        query_down_factor.T, query_up_factor, value_down_factor.T, value_up_factor,
    )
    return pl.pallas_call(
        hand_on_kernel,
        out_shape=[shape(1, T, D), shape(4, R, D, kind=f32)],
        in_specs=[whole()] * 2,
        out_specs=[far()] * 2,
        scratch_shapes=[sem((2,))],
        name="hand_on",
    )(out, merged)


def solution(mesh):
    placed = (P("dp", "seq", None),) * 2 + (P(),) * 9 + (P("dp"),)
    return jax.shard_map(
        per_device,
        mesh=mesh,
        in_specs=placed,
        out_specs=(P("dp", "seq", None), P()),
        check_vma=False,
    )
```
